256 devices in a mesh: dp: 4 (over y), expert: 64 (over x, z, core).
Axes of the slice: x: 4, y: 4, z: 8, core: 2. Of those that a mesh axis runs over, the one named last changes fastest.
Arguments:
- grad_out: bfloat16 [32768, 2048], P(('dp', 'expert')), may hold values from -6 to 6
- layer_input: bfloat16 [32768, 2048], P(('dp', 'expert')), may hold values from -0.8984375 to 0.8984375
- router_weight: bfloat16 [2048, 128], replicated, may hold values from -6 to 6
- gate_probs: float32 [32768, 8], P(('dp', 'expert')), may hold values from 0 to 1, as said below
- expert_ids: int32 [32768, 8], P(('dp', 'expert')), may hold values from 0 to 127, all different within a row; in each aligned block of 128 rows (0 to 127, 128 to 255, ...) at most 9 rows name the same one
- expert_out: bfloat16 [4, 128, 64, 9, 2048], P('dp', 'expert'), may hold values from -0.1875 to 0.1875
Outputs:
- grad_expert_out: bfloat16 [4, 128, 64, 9, 2048], P('dp', 'expert')
- grad_input: bfloat16 [32768, 2048], P(('dp', 'expert'))
- grad_router: float32 [2048, 128], replicated
The draws below stay inside these ranges and needn't reach their ends.
Inputs may be any that keep to these rules, and one draw needn't show every extreme that they name: `expert_ids`: each token names 8 different experts; among the 128 tokens of one device no expert is named more than 9 times, a bound that some block reaches. `gate_probs`: each row is positive and sums to one.
All inputs are finite; a program needn't handle non-finite values.
Results may differ from the reference program's by a relative error of at most 0.012.
Values may be sent and summed in bfloat16 or wider, within the bound.
A program may use at most 128 MiB of HBM per device.

```python
import math
import jax
import jax.numpy as jnp
import numpy as np
from jax import lax

D = 2048
TOP = 8
TOK_DEV = 128
EXPERTS = 128
CAP = 9
TOKENS = 32768
N_DP = 4
N_EXPERT = 64


def draw_gate_probs(key, part):
    key = jax.random.fold_in(key, 5)
    logits = 1.2 * jax.random.normal(key, (TOKENS, TOP), jnp.float32)
    weights = jnp.exp(logits)
    return weights / jnp.sum(weights, axis=-1, keepdims=True)


def levels(key, extent, shards, low, top_value):
    loudness, own = 1.0, jax.random.fold_in(key, 6)
    for axis_at, blocks in shards:
        heights = jnp.exp(jax.random.uniform(jax.random.fold_in(own, axis_at), (blocks,), jnp.float32, low / len(shards), top_value / len(shards)))
        loudness = loudness * jnp.repeat(heights, extent[axis_at] // blocks).reshape([-1 if axis == axis_at else 1 for axis in range(len(extent))])
    return loudness


def shared_out(key, own, number, rows, count, top, reach, lean):
    ranking = jax.random.permutation(key, count)
    crowded, common = portions_of(count, rows * top, reach, lean, True), portions_of(count, rows * top, reach, lean, False)
    places = jnp.arange(count)

    def named(lengths, rotation):
        used = int((lengths > 0).sum())
        fixed = max(1, used // 4)
        moved = fixed + (places - fixed + rotation * (used - fixed)) % max(1, count - fixed)
        return jnp.zeros((count,), jnp.int32).at[ranking[jnp.where(places < fixed, places, moved)]].set(jnp.asarray(lengths, jnp.int32))

    lengths = jnp.where(number % 4 == 0, named(crowded, number // 4), named(common, number - number // 4 - 1))
    mixed = jax.random.permutation(jax.random.fold_in(own, 3), count)
    source_of, receiver = mixed[0:count // 2 * 2:2], mixed[1:count // 2 * 2:2]
    room = jnp.minimum(lengths[source_of] - 1, reach - lengths[receiver]) // 2
    room = jnp.where((source_of == ranking[0]) | (receiver == ranking[0]) | (lengths[receiver] == 0), 0, jnp.maximum(room, 0))
    moved = jax.random.randint(jax.random.fold_in(own, 4), (count // 2,), 0, 1 << 20) % (room + 1)
    lengths = lengths.at[source_of].add(-moved).at[receiver].add(moved)
    labels = jnp.searchsorted(jnp.cumsum(lengths), jnp.arange(rows * top), side="right").astype(jnp.int32)
    listing = labels.reshape(top, rows).T
    listing = listing[jax.random.permutation(jax.random.fold_in(own, 1), rows)]
    rotation = jax.random.randint(jax.random.fold_in(own, 2), (rows, 1), 0, top)
    return jnp.take_along_axis(listing, (jnp.arange(top)[None, :] + rotation) % top, axis=1)


def portions_of(number_of, total, most, skew, full):
    portions = [(1 << 20) // math.isqrt(grade ** skew) + 1 for grade in range(1, number_of + 1)]
    largest = most if full else min(most, max(-(-total // number_of), total * portions[0] // sum(portions)))
    least = 1 if total - largest >= number_of - 1 else 0
    counts, rest = [largest] + [least] * (number_of - 1), total - largest - least * (number_of - 1)
    while rest > 0:
        candidates = [i for i in range(1, number_of) if counts[i] < largest] or [i for i in range(1, number_of) if counts[i] < most]
        mass, left = sum([portions[i] for i in candidates]), rest
        for i in candidates:
            extra = min(most - counts[i], max(1, left * portions[i] // mass), rest)
            counts[i] = counts[i] + extra
            rest = rest - extra
    return np.array(counts)


def centred(stream_key, dims, width, limit, split=(), held_as=jnp.bfloat16):
    array = jax.random.normal(stream_key, dims, jnp.float32) * width
    if len(split) > 0:
        array = levels(stream_key, dims, split, -0.22, 0.18) * array
    return jnp.clip(array, min=-limit, max=limit).astype(held_as)


def setup_inputs(seed: int = 0) -> dict:
    keys = jax.random.split(jax.random.key(seed), 7)
    grad_out = centred(keys[0], (TOKENS, D), 1.0, 6.0, ((0, 256),))
    layer_input = centred(keys[1], (TOKENS, D), 0.15, 0.8984375, ((0, 256),))
    router_weight = centred(keys[2], (D, EXPERTS), 1.0, 6.0)
    gate_probs = draw_gate_probs(jax.random.fold_in(keys[6], 71), 0)
    expert_ids_keys = jax.random.split(jax.random.fold_in(keys[4], 1), TOKENS // TOK_DEV)
    expert_ids_turns = jax.random.permutation(jax.random.fold_in(keys[4], 3), TOKENS // TOK_DEV)
    expert_ids = jax.vmap(lambda own, number: shared_out(jax.random.fold_in(keys[4], 2), own, number, TOK_DEV, EXPERTS, TOP, CAP, 2))(expert_ids_keys, expert_ids_turns).reshape((TOKENS, TOP))
    expert_out = centred(keys[5], (N_DP, EXPERTS, N_EXPERT, CAP, D), 0.03125, 0.1875, ((0, 4), (1, 64)))
    return {"grad_out": grad_out, "layer_input": layer_input, "router_weight": router_weight, "gate_probs": gate_probs, "expert_ids": expert_ids, "expert_out": expert_out}


def slot_table(ids, count):
    flat = ids.reshape(-1)
    onehot = (flat[:, None] == jnp.arange(count, dtype=jnp.int32)[None, :]).astype(jnp.int32)
    before = jnp.cumsum(onehot, axis=0) - onehot
    return jnp.sum(before * onehot, axis=1).reshape(ids.shape).astype(jnp.int32)


def reference(grad_out, layer_input, router_weight, gate_probs, expert_ids, expert_out):
    blocks = N_DP * N_EXPERT
    outs_b = grad_out.reshape(blocks, TOK_DEV, D)
    inputs_b = layer_input.reshape(blocks, TOK_DEV, D)
    gates_b = gate_probs.reshape(blocks, TOK_DEV, TOP)
    ids_b = expert_ids.reshape(blocks, TOK_DEV, TOP)

    def one_block(block):
        group = (block // N_EXPERT).astype(jnp.int32)
        source = (block % N_EXPERT).astype(jnp.int32)
        dout = outs_b[block]
        ids = ids_b[block]
        gates = gates_b[block]
        slot = slot_table(ids, EXPERTS)
        picked = expert_out[group, ids, source, slot]
        grad_gate = jnp.sum(dout.astype(jnp.float32)[:, None, :] * picked.astype(jnp.float32), axis=-1)
        mean_term = jnp.sum(gates * grad_gate, axis=1, keepdims=True)
        grad_score = gates * (grad_gate - mean_term)
        onehot = (ids[:, :, None] == jnp.arange(EXPERTS, dtype=jnp.int32)[None, None, :]).astype(jnp.float32)
        grad_logits = jnp.sum(onehot * grad_score[:, :, None], axis=1).astype(jnp.bfloat16)
        grad_in = jnp.dot(grad_logits, router_weight.T, preferred_element_type=jnp.float32).astype(jnp.bfloat16)
        weight_part = jnp.dot(inputs_b[block].T, grad_logits, preferred_element_type=jnp.float32)
        values = (gates[:, :, None] * dout.astype(jnp.float32)[:, None, :]).astype(jnp.bfloat16)
        grad_y = jnp.zeros((EXPERTS, CAP, D), jnp.bfloat16).at[ids, slot].set(values)
        return grad_in, weight_part, grad_y

    grad_in, weight_parts, grad_y = lax.map(one_block, jnp.arange(blocks, dtype=jnp.int32))
    grad_router = jnp.sum(weight_parts, axis=0)
    grad_expert_out = grad_y.reshape(N_DP, N_EXPERT, EXPERTS, CAP, D).transpose(0, 2, 1, 3, 4)
    return grad_expert_out, grad_in.reshape(TOKENS, D), grad_router
```

```python
import jax
import jax.numpy as jnp
from jax import lax
from jax.experimental import pallas as pl
from jax.experimental.pallas import tpu as pltpu
from jax.sharding import PartitionSpec as P

MESH = pl.DeviceIdType.MESH
BF, F32 = jnp.bfloat16, jnp.float32
NX, NZ, NY = 4, 8, 4
D, TOK, TOP, EXP, CAP = 2048, 128, 8, 128, 9
ROWS = 2 * CAP
PAIRS, SUBS, WID = 4, 2, 256
HOPS = ((4, 3), (3, 4))
REL = ((2, 0), (2, 1), (1, 0), (3, 0), (1, 1), (3, 1), (0, 1), (0, 0))


def iota(shape, axis):
    return lax.broadcasted_iota(jnp.int32, shape, axis)


def dot(a, b, dims=((1,), (0,))):
    return lax.dot_general(a, b, (dims, ((), ())), preferred_element_type=F32)


def earlier():
    return (iota((TOK, TOK), 0) < iota((TOK, TOK), 1)).astype(BF)


def kernel(
    go, li, rw, meta, eo, grows, gin, grout,
    x_buf, o_buf, w_buf, r_buf, e_buf, mb, slots, gates, m_buf, mask,
    own_slot, own_gate, acc, s_out, t_in, lib, lit, glt, glb, part, rb, fin, ag, half, agb,
    loc, xch_s, xch_r, ring_s, ring_r, meta_s, meta_r, li_s, li_r, x_s, x_r,
    sc_s, sc_r, gl_s, gl_r, rs_s, rs_r, a1_s, a1_r, a2_s, a2_r, a3_s, a3_r,
):
    y = lax.axis_index("dp")
    idx = lax.axis_index("expert")
    x, z, c = idx // 16, (idx // 2) % NZ, idx % 2

    def at(dx=0, dy=0, dz=0, dc=0):
        xx, zz, cc = lax.rem(x + dx, NX), lax.rem(z + dz, NZ), lax.rem(c + dc, 2)
        return (lax.rem(y + dy, NY), xx * 16 + zz * 2 + cc)

    def send(src, dst, ss, rs, to):
        return pltpu.make_async_remote_copy(
            src_ref=src, dst_ref=dst, send_sem=ss, recv_sem=rs, device_id=to, device_id_type=MESH
        )

    load_e = pltpu.make_async_copy(eo, e_buf, loc.at[0])
    load_e.start()
    own_half = []
    for p in range(PAIRS):
        cols = pl.ds(pl.multiple_of(c * 1024 + p * WID, WID), WID)
        cp = pltpu.make_async_copy(
            go.at[:, cols], x_buf.at[p, pl.ds((2 * z + c) * TOK, TOK)], loc.at[1 + p]
        )
        cp.start()
        own_half.append(cp)
    own_li = pltpu.make_async_copy(
        li.at[:, pl.ds(pl.multiple_of((2 * y + c) * WID, WID), WID)], lib.at[2 * y + c], loc.at[5]
    )
    own_li.start()
    own_meta = pltpu.make_async_copy(meta, mb.at[pl.ds((2 * z + c) * 16, 16)], loc.at[6])
    own_meta.start()

    barrier = pltpu.get_barrier_semaphore()
    zc = [(dz, dc) for dz in range(NZ) for dc in range(2) if dz or dc]
    yc = [(dy, dc) for dy in range(NY) for dc in range(2) if dy or dc]
    greet = [dict(dz=a, dc=b) for a, b in zc]
    greet += [dict(dx=a, dc=b) for a, b in REL if a]
    greet += [dict(dy=a, dc=b) for a, b in yc if a]
    for g in greet:
        pl.semaphore_signal(barrier, inc=1, device_id=at(**g), device_id_type=MESH)
    pl.semaphore_wait(barrier, len(greet))

    pending = []

    swap = []
    for p in range(PAIRS):
        cols = pl.ds(pl.multiple_of((1 - c) * 1024 + p * WID, WID), WID)
        cp = send(
            go.at[:, cols], x_buf.at[p, pl.ds((2 * z + c) * TOK, TOK)],
            xch_s.at[p], xch_r.at[p], at(dc=1),
        )
        cp.start()
        swap.append(cp)

    meta_cp = []
    for i, (dz, dc) in enumerate(zc):
        cp = send(
            meta, mb.at[pl.ds((2 * z + c) * 16, 16)], meta_s.at[i], meta_r.at[i], at(dz=dz, dc=dc)
        )
        cp.start()
        meta_cp.append(cp)

    def ring(p, s, d, h):
        far = h - 1
        zb = lax.rem(z + (NZ - far if d == 0 else far), NZ)
        blk = x_buf.at[p, pl.ds(zb * 2 * TOK, 2 * TOK), pl.ds(s * 128, 128)]
        return send(
            blk, blk, ring_s.at[p, s, d, h - 1], ring_r.at[p, s, d, h - 1],
            at(dz=1 if d == 0 else NZ - 1),
        )

    def landed(p, s, d, h):
        zb = lax.rem(z + (NZ - h if d == 0 else h), NZ)
        blk = x_buf.at[p, pl.ds(zb * 2 * TOK, 2 * TOK), pl.ds(s * 128, 128)]
        send(
            blk, blk, ring_s.at[p, s, d, h - 1], ring_r.at[p, s, d, h - 1],
            at(dz=1 if d == 0 else NZ - 1),
        ).wait_recv()

    def first(p):
        own_half[p].wait()
        swap[p].wait_recv()
        for s in range(SUBS):
            for d in range(2):
                cp = ring(p, s, d, 1)
                cp.start()
                pending.append(cp)

    def forward(p, s, h):
        for d in range(2):
            if h <= HOPS[s][d]:
                landed(p, s, d, h - 1)
                cp = ring(p, s, d, h)
                cp.start()
                pending.append(cp)

    def finish(p):
        for s in range(SUBS):
            for d in range(2):
                landed(p, s, d, HOPS[s][d])

    first(0)

    li_cp = []
    for i, (dy, dc) in enumerate(yc):
        g = 2 * lax.rem(y + dy, NY) + lax.rem(c + dc, 2)
        cp = send(
            li.at[:, pl.ds(pl.multiple_of(g * WID, WID), WID)], lib.at[2 * y + c],
            li_s.at[i], li_r.at[i], at(dy=dy, dc=dc),
        )
        cp.start()
        li_cp.append(cp)

    lane_row = iota((TOK, TOK), 0)
    expert = 2 * lax.rem(lane_row, 64) + lane_row // 64
    named = jnp.zeros((EXP, TOK), F32)
    gate = jnp.zeros((EXP, TOK), F32)
    for k in range(TOP):
        hit = meta[k : k + 1, :].astype(jnp.int32) == expert
        named = jnp.where(hit, 1.0, named)
        gate = jnp.where(hit, meta[8 + k : 9 + k, :], gate)
    before = dot(named.astype(BF), earlier())
    own_slot[...] = jnp.where(named > 0, before, 99.0)
    own_gate[...] = gate
    for b in range(16):
        mask[:, b * TOK : (b + 1) * TOK] = (iota((16, TOK), 0) == b).astype(BF)

    forward(0, 0, 2)
    forward(0, 1, 2)

    own_meta.wait()
    for cp in meta_cp:
        cp.wait_recv()
    ids = [mb[pl.ds(k, 16, stride=16), :].astype(jnp.int32) for k in range(TOP)]
    gts = [mb[pl.ds(8 + k, 16, stride=16), :] for k in range(TOP)]
    for ei in range(16):
        d, l = ei // 2, ei % 2
        e = (d // 2) * 32 + z * 4 + (d % 2) * 2 + l
        nm = jnp.zeros((16, TOK), F32)
        gt = jnp.zeros((16, TOK), F32)
        for k in range(TOP):
            hit = ids[k] == e
            nm = jnp.where(hit, 1.0, nm)
            gt = jnp.where(hit, gts[k], gt)
        m_buf[ei * 16 : (ei + 1) * 16, :] = nm
        gates[ei * 16 : (ei + 1) * 16, :] = gt
    bef = dot(m_buf[...].astype(BF), earlier())
    slots[...] = jnp.where(m_buf[...] > 0, bef, 99.0)

    def build(lo, hi):
        def one(ei, carry):
            base = pl.multiple_of(ei * 16, 16)
            sl = slots[pl.ds(base, 16), :]
            gt = gates[pl.ds(base, 16), :]
            for s in range(CAP):
                w = jnp.where(sl == float(s), gt, 0.0).astype(BF)
                row = pl.multiple_of(ei * (CAP * 16) + s * 16, 16)
                w_buf[pl.ds(row, 16), :] = jnp.concatenate([w] * 16, axis=1) * mask[...]
            return carry

        lax.fori_loop(lo, hi, one, 0)

    forward(0, 0, 3)
    forward(0, 1, 3)
    build(0, 8)
    first(1)
    forward(0, 0, 4)
    forward(0, 1, 4)
    build(8, 16)
    finish(0)

    def place(p, xs, cs):
        cols = pl.ds(pl.multiple_of(cs * 1024 + p * WID, WID), WID)
        return r_buf.at[:, pl.ds(pl.multiple_of(xs * 16, 16), 16), cols]

    out_cp = []

    def rows(p, a):
        dx, dc = REL[a]
        xd, cd = lax.rem(x + dx, NX), lax.rem(c + dc, 2)
        base = pl.multiple_of((xd * 2 + cd) * (ROWS * 16), 32)
        got = dot(w_buf[pl.ds(base, ROWS * 16), :], x_buf[p])
        o_buf[p, a] = got.astype(BF).reshape(ROWS, 16, WID)
        if a < 7:
            cp = send(o_buf.at[p, a], place(p, x, c), x_s.at[p, a], x_r.at[p, a], at(dx=dx, dc=dc))
            pending.append(cp)
        else:
            cp = pltpu.make_async_copy(o_buf.at[p, a], place(p, x, c), loc.at[7 + p])
            out_cp.append(cp)
        cp.start()

    for p in range(1, PAIRS):
        rows(p - 1, 0)
        forward(p, 0, 2)
        rows(p - 1, 1)
        forward(p, 1, 2)
        rows(p - 1, 2)
        forward(p, 0, 3)
        rows(p - 1, 3)
        forward(p, 1, 3)
        if p + 1 < PAIRS:
            first(p + 1)
        rows(p - 1, 4)
        forward(p, 0, 4)
        rows(p - 1, 5)
        forward(p, 1, 4)
        rows(p - 1, 6)
        rows(p - 1, 7)
        finish(p)
    for a in range(8):
        rows(PAIRS - 1, a)

    own_li.wait()
    for cp in li_cp:
        cp.wait_recv()
    eye = (iota((TOK, TOK), 0) == iota((TOK, TOK), 1)).astype(BF)
    for g in range(8):
        lit[:, g * TOK : (g + 1) * TOK] = dot(lib[g], eye, ((0,), (0,))).astype(BF)

    load_e.wait()
    store_cp = []
    for p in range(PAIRS):
        for a in range(7):
            dx, dc = REL[a]
            xs, cs = lax.rem(x + NX - dx, NX), lax.rem(c + dc, 2)
            send(
                o_buf.at[p, a], place(p, xs, cs), x_s.at[p, a], x_r.at[p, a], at(dx=dx, dc=dc)
            ).wait_recv()
        out_cp[p].wait()
        for h in range(2):
            cols = pl.ds(h * 1024 + p * WID, WID)
            cp = pltpu.make_async_copy(r_buf.at[:, :, cols], grows.at[:, :, cols], loc.at[11 + 2 * p + h])
            cp.start()
            store_cp.append(cp)

        def score(r, carry, p=p):
            tot = jnp.zeros((64, 128), F32)
            for h in range(2):
                for t in range(WID // 128):
                    col = h * 1024 + p * WID + t * 128
                    a = r_buf[r, :, col : col + 128].astype(F32)
                    b = e_buf[r, :, col : col + 128].astype(F32)
                    tot = tot + a * b
            acc[r] = tot if p == 0 else acc[r] + tot
            return carry

        lax.fori_loop(0, ROWS, score, 0)

    total = jnp.zeros((64, 128), F32)
    for r in range(ROWS):
        total = jnp.where(iota((64, 128), 1) == r, jnp.sum(acc[r], axis=1, keepdims=True), total)
    s_out[...] = total.reshape(64, 1, 128)

    def sc(i):
        to = lax.rem(idx + i, 64)
        return send(s_out.at[to], t_in.at[idx], sc_s.at[i], sc_r.at[i], (y, to))

    def sc_start(i, carry):
        sc(i).start()
        return carry

    def sc_wait(i, carry):
        fr = lax.rem(idx + 64 - i, 64)
        send(s_out.at[fr], t_in.at[fr], sc_s.at[i], sc_r.at[i], (y, fr)).wait_recv()
        return carry

    lax.fori_loop(1, 64, sc_start, 0)
    t_in[pl.ds(idx, 1)] = s_out[pl.ds(idx, 1)]
    lax.fori_loop(1, 64, sc_wait, 0)

    back = t_in[...].reshape(64, 128)
    scaled = []
    for l in range(2):
        sl = own_slot[l * 64 : (l + 1) * 64, :]
        v = jnp.zeros((64, TOK), F32)
        for s in range(CAP):
            v = jnp.where(sl == float(s), back[:, l * CAP + s : l * CAP + s + 1], v)
        scaled.append(v)
    scaled = jnp.concatenate(scaled, axis=0)
    logits = scaled - own_gate[...] * jnp.sum(scaled, axis=0, keepdims=True)
    order = (2 * lax.rem(lane_row, 64) + lane_row // 64 == iota((TOK, TOK), 1)).astype(BF)
    glt[...] = dot(logits.astype(BF), order, ((0,), (0,))).astype(BF)

    gl_cp = []
    for i, (dy, dc) in enumerate(yc):
        cp = send(glt, glb.at[2 * y + c], gl_s.at[i], gl_r.at[i], at(dy=dy, dc=dc))
        cp.start()
        gl_cp.append(cp)
    glb[pl.ds(2 * y + c, 1)] = glt[...].reshape(1, TOK, EXP)
    gin[...] = dot(glt[...], rw[...], ((1,), (1,))).astype(BF)
    for cp in gl_cp:
        cp.wait_recv()
    part[...] = dot(lit[...], glb[...].reshape(8 * TOK, EXP))

    chip = x * NZ + z

    def chip_at(i):
        q = lax.rem(chip + i, 32)
        return q, (y, q * 2 + c)

    def rs_start(i, carry):
        q, to = chip_at(i)
        send(
            part.at[pl.ds(pl.multiple_of(q * 8, 8), 8)], rb.at[chip], rs_s.at[i], rs_r.at[i], to
        ).start()
        return carry

    def rs_wait(i, carry):
        q, to = chip_at(32 - i)
        send(
            part.at[pl.ds(pl.multiple_of(q * 8, 8), 8)], rb.at[q], rs_s.at[i], rs_r.at[i], to
        ).wait_recv()
        return carry

    lax.fori_loop(1, 32, rs_start, 0)
    rb[pl.ds(chip, 1)] = part[pl.ds(pl.multiple_of(chip * 8, 8), 8), :].reshape(1, 8, EXP)
    lax.fori_loop(1, 32, rs_wait, 0)
    fin[...] = jnp.sum(rb[...], axis=0)

    def a1_start(i, carry):
        q, to = chip_at(i)
        send(fin, ag.at[chip], a1_s.at[i], a1_r.at[i], to).start()
        return carry

    def a1_wait(i, carry):
        q, to = chip_at(32 - i)
        send(fin, ag.at[q], a1_s.at[i], a1_r.at[i], to).wait_recv()
        return carry

    lax.fori_loop(1, 32, a1_start, 0)
    ag[pl.ds(chip, 1)] = fin[...].reshape(1, 8, EXP)
    lax.fori_loop(1, 32, a1_wait, 0)
    half[...] = ag[...].reshape(256, EXP).astype(BF)

    a2_cp = []
    for i in range(1, NY):
        cp = send(half, agb.at[2 * y + c], a2_s.at[i], a2_r.at[i], at(dy=i))
        cp.start()
        a2_cp.append(cp)
    a3_cp = []

    def swap_part(i, g, src):
        cp = send(src, agb.at[g], a3_s.at[i], a3_r.at[i], at(dc=1))
        cp.start()
        a3_cp.append(cp)

    swap_part(0, 2 * y + c, half)
    agb[pl.ds(2 * y + c, 1)] = half[...].reshape(1, 256, EXP)
    for i in range(1, NY):
        ys = lax.rem(y + NY - i, NY)
        send(half, agb.at[2 * ys + c], a2_s.at[i], a2_r.at[i], at(dy=i)).wait_recv()
        swap_part(i, 2 * ys + c, agb.at[2 * ys + c])
    for i in range(NY):
        ys = lax.rem(y + NY - i, NY)
        g = 2 * ys + 1 - c
        send(half, agb.at[g], a3_s.at[i], a3_r.at[i], at(dc=1)).wait_recv()
    grout[...] = agb[...].reshape(D, EXP).astype(F32)

    for cp in swap + meta_cp + pending + li_cp + gl_cp + a2_cp + a3_cp:
        cp.wait_send()

    def sc_left(i, carry):
        sc(i).wait_send()
        return carry

    def rs_left(i, carry):
        q, to = chip_at(i)
        send(
            part.at[pl.ds(pl.multiple_of(q * 8, 8), 8)], rb.at[chip], rs_s.at[i], rs_r.at[i], to
        ).wait_send()
        send(fin, ag.at[chip], a1_s.at[i], a1_r.at[i], to).wait_send()
        return carry

    lax.fori_loop(1, 64, sc_left, 0)
    lax.fori_loop(1, 32, rs_left, 0)
    for cp in store_cp:
        cp.wait()


def body(grad_out, layer_input, router_weight, gate_probs, expert_ids, expert_out):
    meta = jnp.concatenate([expert_ids.T.astype(F32), gate_probs.T], axis=0)
    eo = expert_out[0].transpose(0, 2, 1, 3).reshape(ROWS, 64, D)
    vm, sem = pltpu.VMEM, pltpu.SemaphoreType.DMA
    hbm = pl.BlockSpec(memory_space=pl.ANY)
    vmem = pl.BlockSpec(memory_space=pltpu.VMEM)
    grows, gin, grout = pl.pallas_call(
        kernel,
        out_shape=(
            jax.ShapeDtypeStruct((ROWS, 64, D), BF),
            jax.ShapeDtypeStruct((TOK, D), BF),
            jax.ShapeDtypeStruct((D, EXP), F32),
        ),
        in_specs=[vmem, vmem, vmem, vmem, hbm],
        out_specs=(hbm, vmem, vmem),
        scratch_shapes=[
            vm((PAIRS, 16 * TOK, WID), BF),
            vm((PAIRS, 8, ROWS, 16, WID), BF),
            vm((8 * ROWS * 16, 16 * TOK), BF),
            vm((ROWS, 64, D), BF),
            vm((ROWS, 64, D), BF),
            vm((256, TOK), F32),
            vm((256, TOK), F32),
            vm((256, TOK), F32),
            vm((256, TOK), F32),
            vm((16, 16 * TOK), BF),
            vm((EXP, TOK), F32),
            vm((EXP, TOK), F32),
            vm((ROWS, 64, 128), F32),
            vm((64, 1, 128), F32),
            vm((64, 1, 128), F32),
            vm((8, TOK, WID), BF),
            vm((WID, 8 * TOK), BF),
            vm((TOK, EXP), BF),
            vm((8, TOK, EXP), BF),
            vm((WID, EXP), F32),
            vm((32, 8, EXP), F32),
            vm((8, EXP), F32),
            vm((32, 8, EXP), F32),
            vm((256, EXP), BF),
            vm((8, 256, EXP), BF),
            sem((19,)),
            sem((PAIRS,)), sem((PAIRS,)),
            sem((PAIRS, SUBS, 2, 4)), sem((PAIRS, SUBS, 2, 4)),
            sem((15,)), sem((15,)),
            sem((7,)), sem((7,)),
            sem((PAIRS, 7)), sem((PAIRS, 7)),
            sem((64,)), sem((64,)),
            sem((7,)), sem((7,)),
            sem((32,)), sem((32,)),
            sem((32,)), sem((32,)),
            sem((NY,)), sem((NY,)),
            sem((NY,)), sem((NY,)),
        ],
        compiler_params=pltpu.CompilerParams(
            collective_id=0, has_side_effects=True, vmem_limit_bytes=52 * 2**20
        ),
    )(grad_out, layer_input, router_weight, meta, eo)
    grows = grows.reshape(2, CAP, 64, D).transpose(0, 2, 1, 3)
    return grows[None], gin, grout


def solution(mesh):
    return jax.shard_map(
        body,
        mesh=mesh,
        in_specs=(
            P(("dp", "expert"), None),
            P(("dp", "expert"), None),
            P(),
            P(("dp", "expert"), None),
            P(("dp", "expert"), None),
            P("dp", "expert", None, None, None),
        ),
        out_specs=(P("dp", "expert", None, None, None), P(("dp", "expert"), None), P()),
        check_vma=False,
    )
```

```python
import jax
import jax.numpy as jnp
from jax import lax
from jax.experimental import pallas as pl
from jax.experimental.pallas import tpu as pltpu
from jax.sharding import PartitionSpec as P

MESH = pl.DeviceIdType.MESH
BF, F32 = jnp.bfloat16, jnp.float32
NX, NZ, NY = 4, 8, 4
D, TOK, TOP, EXP, CAP = 2048, 128, 8, 128, 9
ROWS = 2 * CAP
UNITS, UW, WID = 8, 128, 256
HOPS = ((4, 3), (3, 4))
STEP, HOP = 5.8, 3.3
REL = ((2, 0), (2, 1), (1, 0), (3, 0), (1, 1), (3, 1), (0, 1), (0, 0))


def iota(shape, axis):
    return lax.broadcasted_iota(jnp.int32, shape, axis)


def dot(a, b, dims=((1,), (0,))):
    return lax.dot_general(a, b, (dims, ((), ())), preferred_element_type=F32)


def earlier():
    return (iota((TOK, TOK), 0) < iota((TOK, TOK), 1)).astype(BF)


def kernel(
    go, li, rw_in, ids_in, gates_in, eo, grows, gin_out, agb_out,
    x_buf, f_buf, o_buf, w_buf, r_buf, gin, agb, e_buf, rw, ids_own, gates_own, meta, mb, slots, gates, m_buf,
    own_slot, own_gate, acc, s_out, t_in, lib, lit, glt, glb, part, rb, fin, ag, half,
    loc, xch_s, xch_r, ring_s, ring_r, meta_s, meta_r, li_s, li_r, x_s, x_r,
    sc_s, sc_r, gl_s, gl_r, rs_s, rs_r, a1_s, a1_r, a2_s, a2_r, a3_s, a3_r,
):
    y = lax.axis_index("dp")
    idx = lax.axis_index("expert")
    x, z, c = idx // 16, (idx // 2) % NZ, idx % 2

    def at(dx=0, dy=0, dz=0, dc=0):
        xx, zz, cc = lax.rem(x + dx, NX), lax.rem(z + dz, NZ), lax.rem(c + dc, 2)
        return (lax.rem(y + dy, NY), xx * 16 + zz * 2 + cc)

    def bulk(ref, n, s):
        pltpu.make_async_copy(ref.at[pl.ds(0, n)], ref.at[pl.ds(0, n)], s).wait()

    def send(src, dst, ss, rs, to):
        return pltpu.make_async_remote_copy(
            src_ref=src, dst_ref=dst, send_sem=ss, recv_sem=rs, device_id=to, device_id_type=MESH
        )

    load_ids = pltpu.make_async_copy(ids_in, ids_own, loc.at[6])
    load_ids.start()
    load_gates = pltpu.make_async_copy(gates_in, gates_own, loc.at[11])
    load_gates.start()
    load_e = pltpu.make_async_copy(eo, e_buf, loc.at[0])
    load_e.start()
    own_half = []
    for u in range(UNITS):
        cols = pl.ds(pl.multiple_of(c * 1024 + u * UW, UW), UW)
        cp = pltpu.make_async_copy(go.at[:, cols], x_buf.at[u, 2 * z + c], loc.at[13 + u])
        cp.start()
        own_half.append(cp)
    own_li = pltpu.make_async_copy(
        li.at[:, pl.ds(pl.multiple_of((2 * y + c) * WID, WID), WID)], lib.at[2 * y + c], loc.at[5]
    )
    own_li.start()
    load_rw = pltpu.make_async_copy(rw_in, rw, loc.at[12])
    load_rw.start()

    barrier = pltpu.get_barrier_semaphore()
    zc = [(dz, dc) for dz in range(NZ) for dc in range(2) if dz or dc]
    yc = [(dy, dc) for dy in range(NY) for dc in range(2) if dy or dc]
    greet = [dict(dz=a, dc=b) for a, b in zc]
    greet += [dict(dx=a, dc=b) for a, b in REL if a]
    greet += [dict(dy=a, dc=b) for a, b in yc if a]
    for g in greet:
        pl.semaphore_signal(barrier, inc=1, device_id=at(**g), device_id_type=MESH)
    load_ids.wait()
    load_gates.wait()
    meta[0:TOP, :] = ids_own[...].astype(F32).astype(BF)
    meta[TOP:, :] = gates_own[...].astype(BF)
    mb[pl.ds(2 * z + c, 1)] = meta[...].reshape(1, 2 * TOP, TOK)
    pl.semaphore_wait(barrier, len(greet))

    pending = []

    swap = []
    for u in range(UNITS):
        cols = pl.ds(pl.multiple_of((1 - c) * 1024 + u * UW, UW), UW)
        swap.append(
            send(go.at[:, cols], x_buf.at[u, 2 * z + c], xch_s.at[u], xch_r.at[u], at(dc=1))
        )
    swap[0].start()
    swap[1].start()

    def came(d, h):
        return lax.rem(z + (NZ - h if d == 0 else h), NZ)

    def ring(u, d, h):
        blk = x_buf.at[u, pl.ds(2 * came(d, h - 1), 2)]
        return send(
            blk, blk, ring_s.at[u, d, h - 1], ring_r.at[u, d, h - 1],
            at(dz=1 if d == 0 else NZ - 1),
        )

    def landed(u, d, h):
        blk = x_buf.at[u, pl.ds(2 * came(d, h), 2)]
        send(
            blk, blk, ring_s.at[u, d, h - 1], ring_r.at[u, d, h - 1],
            at(dz=1 if d == 0 else NZ - 1),
        ).wait_recv()

    def hop(u, h):
        if h == 0:
            own_half[u].wait()
            swap[u].wait_recv()
        for d in range(2):
            if 0 < h <= HOPS[u % 2][d]:
                landed(u, d, h)
            if h < HOPS[u % 2][d]:
                cp = ring(u, d, h + 1)
                cp.start()
                pending.append(cp)

    steps = sorted((u * STEP + h * HOP, u, h) for u in range(UNITS) for h in range(5))
    steps = [(u, h) for _, u, h in steps]
    hop(*steps[0])

    meta_cp = []
    for i, (dz, dc) in enumerate(zc):
        cp = send(meta, mb.at[2 * z + c], meta_s.at[i], meta_r.at[i], at(dz=dz, dc=dc))
        cp.start()
        meta_cp.append(cp)
    for u in range(2, UNITS):
        swap[u].start()

    lane_row = iota((TOK, TOK), 0)
    expert = 2 * lax.rem(lane_row, 64) + lane_row // 64
    named = jnp.zeros((EXP, TOK), F32)
    gate = jnp.zeros((EXP, TOK), F32)
    for k in range(TOP):
        hit = ids_own[k : k + 1, :] == expert
        named = jnp.where(hit, 1.0, named)
        gate = jnp.where(hit, gates_own[k : k + 1, :], gate)
    before = dot(named.astype(BF), earlier())
    own_slot[...] = jnp.where(named > 0, before, 99.0)
    own_gate[...] = gate

    li_cp = []
    for i, (dy, dc) in enumerate(yc):
        g = 2 * lax.rem(y + dy, NY) + lax.rem(c + dc, 2)
        cp = send(
            li.at[:, pl.ds(pl.multiple_of(g * WID, WID), WID)], lib.at[2 * y + c],
            li_s.at[i], li_r.at[i], at(dy=dy, dc=dc),
        )
        li_cp.append(cp)

    def tables():
        for cp in meta_cp:
            cp.wait_recv()
        row = iota((16, TOK), 0)
        here = (row // 4) * 32 + z * 4 + lax.rem(row, 4)
        for j in range(16):
            ids = mb[j, 0:TOP, :].astype(F32).astype(jnp.int32)
            gts = mb[j, TOP:, :].astype(F32)
            nm = jnp.zeros((16, TOK), F32)
            gt = jnp.zeros((16, TOK), F32)
            for k in range(TOP):
                hit = ids[k : k + 1, :] == here
                nm = jnp.where(hit, 1.0, nm)
                gt = jnp.where(hit, gts[k : k + 1, :], gt)
            m_buf[j * 16 : (j + 1) * 16, :] = nm
            gates[j * 16 : (j + 1) * 16, :] = gt
        bef = dot(m_buf[...].astype(BF), earlier())
        slots[...] = jnp.where(m_buf[...] > 0, bef, 99.0)

        def one(j, carry):
            base = pl.multiple_of(j * 16, 16)
            sl = slots[pl.ds(base, 16), :]
            gt = gates[pl.ds(base, 16), :]
            for s in range(CAP):
                w_buf[j, s * 16 : (s + 1) * 16, :] = jnp.where(sl == float(s), gt, 0.0).astype(BF)
            return carry

        lax.fori_loop(0, 16, one, 0)

    def block(u, zb):
        for i in range(2):
            j = 2 * zb + i
            got = dot(w_buf[j], x_buf[u, j])
            for s in range(CAP):
                f_buf[u % 4, pl.ds(s * 16 + j, 16, stride=CAP * 16), :] = got[s * 16 : (s + 1) * 16, :]

    def place(u, xs, cs):
        cols = pl.ds(pl.multiple_of(cs * 1024 + u * UW, UW), UW)
        return r_buf.at[:, pl.ds(pl.multiple_of(xs * 16, 16), 16), cols]

    out_cp = []

    def rows(u, a):
        dx, dc = REL[a]
        xd, cd = lax.rem(x + dx, NX), lax.rem(c + dc, 2)
        base = pl.multiple_of((xd * 2 + cd) * (ROWS * 16), 32)
        o_buf[u, a] = f_buf[u % 4, pl.ds(base, ROWS * 16), :].astype(BF).reshape(ROWS, 16, UW)
        if a < 7:
            cp = send(o_buf.at[u, a], place(u, x, c), x_s.at[u, a], x_r.at[u, a], at(dx=dx, dc=dc))
            pending.append(cp)
        else:
            cp = pltpu.make_async_copy(o_buf.at[u, a], place(u, x, c), loc.at[21 + u])
            out_cp.append(cp)
        cp.start()

    def work(u, h):
        if h == 0:
            block(u, z)
        for d in range(2):
            if 0 < h <= HOPS[u % 2][d]:
                block(u, came(d, h))
        if h == 4:
            for a in range(8):
                rows(u, a)

    late = [steps[0]]
    for n, (u, h) in enumerate(steps[1:]):
        hop(u, h)
        late.append((u, h))
        if n == 2:
            for cp in li_cp:
                cp.start()
            tables()
        if n >= 2:
            for q in late:
                work(*q)
            late = []

    own_li.wait()
    for cp in li_cp:
        cp.wait_recv()
    eye = (iota((TOK, TOK), 0) == iota((TOK, TOK), 1)).astype(BF)
    for g in range(8):
        lit[:, g * TOK : (g + 1) * TOK] = dot(lib[g], eye, ((0,), (0,))).astype(BF)

    load_e.wait()
    store_cp = []
    for u in range(UNITS):
        for a in range(7):
            dx, dc = REL[a]
            xs, cs = lax.rem(x + NX - dx, NX), lax.rem(c + dc, 2)
            send(
                o_buf.at[u, a], place(u, xs, cs), x_s.at[u, a], x_r.at[u, a], at(dx=dx, dc=dc)
            ).wait_recv()
        out_cp[u].wait()
        for h in range(2):
            cols = pl.ds(h * 1024 + u * UW, UW)
            cp = pltpu.make_async_copy(r_buf.at[:, :, cols], grows.at[:, :, cols], loc.at[29 + 2 * u + h])
            cp.start()
            store_cp.append(cp)

        def score(r, carry, u=u):
            tot = jnp.zeros((64, 128), F32)
            for h in range(2):
                col = h * 1024 + u * UW
                a = r_buf[r, :, col : col + 128].astype(F32)
                b = e_buf[r, :, col : col + 128].astype(F32)
                tot = tot + a * b
            acc[r] = tot if u == 0 else acc[r] + tot
            return carry

        lax.fori_loop(0, ROWS, score, 0)

    total = jnp.zeros((64, 128), F32)
    for r in range(ROWS):
        total = jnp.where(iota((64, 128), 1) == r, jnp.sum(acc[r], axis=1, keepdims=True), total)
    s_out[...] = total.reshape(64, 1, 128)

    def sc(i):
        to = lax.rem(idx + i, 64)
        return send(s_out.at[to], t_in.at[idx], sc_s, sc_r, (y, to))

    def sc_start(i, carry):
        sc(i).start()
        return carry

    lax.fori_loop(1, 64, sc_start, 0)
    t_in[pl.ds(idx, 1)] = s_out[pl.ds(idx, 1)]
    for cp in swap + meta_cp + pending + li_cp:
        cp.wait_send()
    bulk(t_in, 63, sc_r)

    back = t_in[...].reshape(64, 128)
    scaled = []
    for l in range(2):
        sl = own_slot[l * 64 : (l + 1) * 64, :]
        v = jnp.zeros((64, TOK), F32)
        for s in range(CAP):
            v = jnp.where(sl == float(s), back[:, l * CAP + s : l * CAP + s + 1], v)
        scaled.append(v)
    scaled = jnp.concatenate(scaled, axis=0)
    logits = scaled - own_gate[...] * jnp.sum(scaled, axis=0, keepdims=True)
    order = (2 * lax.rem(lane_row, 64) + lane_row // 64 == iota((TOK, TOK), 1)).astype(BF)
    glt[...] = dot(logits.astype(BF), order, ((0,), (0,))).astype(BF)

    gl_cp = []
    for i, (dy, dc) in enumerate(yc):
        cp = send(glt, glb.at[2 * y + c], gl_s.at[i], gl_r.at[i], at(dy=dy, dc=dc))
        cp.start()
        gl_cp.append(cp)
    glb[pl.ds(2 * y + c, 1)] = glt[...].reshape(1, TOK, EXP)
    load_rw.wait()
    gin[...] = dot(glt[...], rw[...], ((1,), (1,))).astype(BF)
    cp = pltpu.make_async_copy(gin, gin_out, loc.at[1])
    cp.start()
    store_cp.append(cp)
    for cp in gl_cp:
        cp.wait_recv()
    part[...] = dot(lit[...], glb[...].reshape(8 * TOK, EXP))

    chip = x * NZ + z

    def chip_at(i):
        q = lax.rem(chip + i, 32)
        return q, (y, q * 2 + c)

    def rs_start(i, carry):
        q, to = chip_at(i)
        send(
            part.at[pl.ds(pl.multiple_of(q * 8, 8), 8)], rb.at[chip], rs_s, rs_r, to
        ).start()
        return carry

    lax.fori_loop(1, 32, rs_start, 0)
    rb[pl.ds(chip, 1)] = part[pl.ds(pl.multiple_of(chip * 8, 8), 8), :].reshape(1, 8, EXP)
    bulk(s_out, 63, sc_s)
    for cp in gl_cp:
        cp.wait_send()
    bulk(rb, 31, rs_r)
    fin[...] = jnp.sum(rb[...], axis=0)

    def a1_start(i, carry):
        q, to = chip_at(i)
        send(fin, ag.at[chip], a1_s, a1_r, to).start()
        return carry

    lax.fori_loop(1, 32, a1_start, 0)
    ag[pl.ds(chip, 1)] = fin[...].reshape(1, 8, EXP)
    bulk(rb, 31, rs_s)
    bulk(ag, 31, a1_r)
    half[...] = ag[...].reshape(256, EXP).astype(BF)

    a2_cp = []
    for i in range(1, NY):
        cp = send(half, agb.at[2 * y + c], a2_s.at[i], a2_r.at[i], at(dy=i))
        cp.start()
        a2_cp.append(cp)
    a3_cp = []

    def swap_part(i, g, src):
        cp = send(src, agb.at[g], a3_s.at[i], a3_r.at[i], at(dc=1))
        cp.start()
        a3_cp.append(cp)

    swap_part(0, 2 * y + c, half)
    agb[pl.ds(2 * y + c, 1)] = half[...].reshape(1, 256, EXP)
    bulk(ag, 31, a1_s)
    for cp in store_cp:
        cp.wait()
    for i in range(1, NY):
        ys = lax.rem(y + NY - i, NY)
        send(half, agb.at[2 * ys + c], a2_s.at[i], a2_r.at[i], at(dy=i)).wait_recv()
        swap_part(i, 2 * ys + c, agb.at[2 * ys + c])
    for i in range(NY):
        ys = lax.rem(y + NY - i, NY)
        g = 2 * ys + 1 - c
        send(half, agb.at[g], a3_s.at[i], a3_r.at[i], at(dc=1)).wait_recv()

    store = pltpu.make_async_copy(agb, agb_out, loc.at[0])
    store.start()
    for cp in a2_cp + a3_cp:
        cp.wait_send()
    store.wait()


def writer(rows_in, gin_in, agb_in, grows, gin_out, grout, rows, gin, parts, wide, loc, sto):
    pieces = [(rows_in.at[pl.ds(3 * i, 3)], rows.at[pl.ds(3 * i, 3)], grows.at[pl.ds(3 * i, 3)]) for i in range(6)]
    pieces.append((gin_in, gin, gin_out))
    load = pltpu.make_async_copy(agb_in, parts, loc.at[7])
    load.start()
    loads = [pltpu.make_async_copy(a, b, loc.at[i]) for i, (a, b, _) in enumerate(pieces)]
    stores = [pltpu.make_async_copy(b, c, sto.at[i]) for i, (_, b, c) in enumerate(pieces)]
    for cp in loads:
        cp.start()
    load.wait()
    wide[...] = parts[...].reshape(D, EXP).astype(F32)
    stores.append(pltpu.make_async_copy(wide, grout, sto.at[7]))
    stores[7].start()
    for i in range(7):
        loads[i].wait()
        stores[i].start()
    for cp in stores:
        cp.wait()


def body(grad_out, layer_input, router_weight, gate_probs, expert_ids, expert_out):
    eo = expert_out[0].transpose(0, 2, 1, 3).reshape(ROWS, 64, D)
    vm, sem = pltpu.VMEM, pltpu.SemaphoreType.DMA
    hbm = pl.BlockSpec(memory_space=pltpu.HBM)
    results = pl.pallas_call(
        kernel,
        out_shape=(
            jax.ShapeDtypeStruct((ROWS, 64, D), BF),
            jax.ShapeDtypeStruct((TOK, D), BF),
            jax.ShapeDtypeStruct((8, 256, EXP), BF),
        ),
        in_specs=[hbm] * 6,
        out_specs=(hbm, hbm, hbm),
        scratch_shapes=[
            vm((UNITS, 16, TOK, UW), BF),
            vm((4, 8 * ROWS * 16, UW), F32),
            vm((UNITS, 8, ROWS, 16, UW), BF),
            vm((16, CAP * 16, TOK), BF),
            vm((ROWS, 64, D), BF),
            vm((TOK, D), BF),
            vm((8, 256, EXP), BF),
            vm((ROWS, 64, D), BF),
            vm((D, EXP), BF),
            vm((TOP, TOK), jnp.int32),
            vm((TOP, TOK), F32),
            vm((2 * TOP, TOK), BF),
            vm((16, 2 * TOP, TOK), BF),
            vm((256, TOK), F32),
            vm((256, TOK), F32),
            vm((256, TOK), F32),
            vm((EXP, TOK), F32),
            vm((EXP, TOK), F32),
            vm((ROWS, 64, 128), F32),
            vm((64, 1, 128), F32),
            vm((64, 1, 128), F32),
            vm((8, TOK, WID), BF),
            vm((WID, 8 * TOK), BF),
            vm((TOK, EXP), BF),
            vm((8, TOK, EXP), BF),
            vm((WID, EXP), F32),
            vm((32, 8, EXP), F32),
            vm((8, EXP), F32),
            vm((32, 8, EXP), F32),
            vm((256, EXP), BF),
            sem((45,)),
            sem((UNITS,)), sem((UNITS,)),
            sem((UNITS, 2, 4)), sem((UNITS, 2, 4)),
            sem((15,)), sem((15,)),
            sem((7,)), sem((7,)),
            sem((UNITS, 7)), sem((UNITS, 7)),
            sem, sem,
            sem((7,)), sem((7,)),
            sem, sem,
            sem, sem,
            sem((NY,)), sem((NY,)),
            sem((NY,)), sem((NY,)),
        ],
        compiler_params=pltpu.CompilerParams(
            collective_id=0, has_side_effects=True, vmem_limit_bytes=57 * 2**20
        ),
    )(grad_out, layer_input, router_weight, expert_ids.T, gate_probs.T, eo)
    grows, gin, grout = pl.pallas_call(
        writer,
        out_shape=(
            jax.ShapeDtypeStruct((ROWS, 64, D), BF),
            jax.ShapeDtypeStruct((TOK, D), BF),
            jax.ShapeDtypeStruct((D, EXP), F32),
        ),
        in_specs=[hbm] * 3,
        out_specs=(hbm, hbm, hbm),
        scratch_shapes=[
            vm((ROWS, 64, D), BF), vm((TOK, D), BF), vm((8, 256, EXP), BF), vm((D, EXP), F32),
            sem((8,)), sem((8,)),
        ],
        compiler_params=pltpu.CompilerParams(vmem_limit_bytes=57 * 2**20),
    )(*results)
    grows = grows.reshape(2, CAP, 64, D).transpose(0, 2, 1, 3)
    return grows[None], gin, grout


def solution(mesh):
    return jax.shard_map(
        body,
        mesh=mesh,
        in_specs=(
            P(("dp", "expert"), None),
            P(("dp", "expert"), None),
            P(),
            P(("dp", "expert"), None),
            P(("dp", "expert"), None),
            P("dp", "expert", None, None, None),
        ),
        out_specs=(P("dp", "expert", None, None, None), P(("dp", "expert"), None), P()),
        check_vma=False,
    )
```

```python
import jax
import jax.numpy as jnp
from jax import lax
from jax.experimental import pallas as pl
from jax.experimental.pallas import tpu as pltpu
from jax.sharding import PartitionSpec as P

MESH = pl.DeviceIdType.MESH
BF, F32 = jnp.bfloat16, jnp.float32
NX, NZ, NY = 4, 8, 4
D, TOK, TOP, EXP, CAP = 2048, 128, 8, 128, 9
ROWS = 2 * CAP
UNITS, UW, WID = 8, 128, 256
RING = 7
HOPS = ((4, 3), (3, 4))
STEP, HOP = 4.8, 3.3
ORDER = (0, 1, 2, 3, 4, 5, 7, 6)
ACROSS = tuple((dz, dc) for dz in (4, 3, 5, 2, 6, 1, 7) for dc in range(2)) + ((0, 1),)
SPREAD = (0, 0, 0, 0, 0, 5, 10)
REL = ((2, 0), (2, 1), (1, 0), (3, 0), (1, 1), (3, 1), (0, 1), (0, 0))


def iota(shape, axis):
    return lax.broadcasted_iota(jnp.int32, shape, axis)


def dot(a, b, dims=((1,), (0,))):
    return lax.dot_general(a, b, (dims, ((), ())), preferred_element_type=F32)


def earlier():
    return (iota((TOK, TOK), 0) < iota((TOK, TOK), 1)).astype(BF)


def kernel(
    go, li, rw_in, ids_in, gates_in, eo, grows, gin_out, agb_out,
    x_buf, f_buf, o_buf, w_buf, r_buf, gin, agb, e_buf, rw, ids_own, gates_own, meta, mb, slots, gates, m_buf, mb2, g2_buf, w2_buf, f2_buf, o2_buf, h_in, turn, order,
    own_slot, own_gate, acc, s_out, t_in, lib, lit, glt, glb, part, rb, fin, ag, half,
    loc, xch_s, xch_r, ring_s, ring_r, meta_s, meta_r, li_s, li_r, x_s, x_r, h_s, h_r, h2_s, h2_r, h3_s, h3_r,
    sc_s, sc_r, gl_s, gl_r, rs_s, rs_r, a1_s, a1_r, a2_s, a2_r, a3_s, a3_r,
):
    y = lax.axis_index("dp")
    idx = lax.axis_index("expert")
    x, z, c = idx // 16, (idx // 2) % NZ, idx % 2

    def at(dx=0, dy=0, dz=0, dc=0):
        xx, zz, cc = lax.rem(x + dx, NX), lax.rem(z + dz, NZ), lax.rem(c + dc, 2)
        return (lax.rem(y + dy, NY), xx * 16 + zz * 2 + cc)

    def bulk(ref, n, s):
        pltpu.make_async_copy(ref.at[pl.ds(0, n)], ref.at[pl.ds(0, n)], s).wait()

    def taken(ref, s):
        pltpu.make_async_copy(ref, ref, s).wait()

    def send(src, dst, ss, rs, to):
        return pltpu.make_async_remote_copy(
            src_ref=src, dst_ref=dst, send_sem=ss, recv_sem=rs, device_id=to, device_id_type=MESH
        )

    load_ids = pltpu.make_async_copy(ids_in, ids_own, loc.at[6])
    load_ids.start()
    load_gates = pltpu.make_async_copy(gates_in, gates_own, loc.at[2])
    load_gates.start()
    load_e = pltpu.make_async_copy(eo, e_buf, loc.at[0])
    load_e.start()
    own_half = []
    for u in range(UNITS):
        cols = pl.ds(pl.multiple_of(c * 1024 + u * UW, UW), UW)
        cp = pltpu.make_async_copy(go.at[:, cols], x_buf.at[u, 2 * z + c], loc.at[7 + u])
        cp.start()
        own_half.append(cp)
    own_li = pltpu.make_async_copy(
        li.at[:, pl.ds(pl.multiple_of((2 * y + c) * WID, WID), WID)], lib.at[2 * y + c], loc.at[5]
    )
    own_li.start()
    load_rw = pltpu.make_async_copy(rw_in, rw, loc.at[3])
    load_rw.start()

    barrier = pltpu.get_barrier_semaphore()
    zc = [(dz, dc) for dz in range(NZ) for dc in range(2) if dz or dc]
    yc = [(dy, dc) for dy in range(NY) for dc in range(2) if dy or dc]
    greet = [dict(dz=a, dc=b) for a, b in zc]
    greet += [dict(dx=a, dc=b) for a, b in REL if a]
    greet += [dict(dy=a, dc=b) for a, b in yc if a]
    for g in greet:
        pl.semaphore_signal(barrier, inc=1, device_id=at(**g), device_id_type=MESH)
    load_ids.wait()
    load_gates.wait()
    meta[0:TOP, :] = ids_own[...].astype(F32).astype(BF)
    meta[TOP:, :] = gates_own[...].astype(BF)
    mb[pl.ds(2 * z + c, 1)] = meta[...].reshape(1, 2 * TOP, TOK)
    pl.semaphore_wait(barrier, len(greet))


    swap = []
    for u in range(UNITS):
        cols = pl.ds(pl.multiple_of((1 - c) * 1024 + u * UW, UW), UW)
        swap.append(
            send(go.at[:, cols], x_buf.at[u, 2 * z + c], xch_s, xch_r.at[u], at(dc=1))
        )
    swap[0].start()
    swap[RING].start()
    swap[1].start()

    def came(d, h):
        return lax.rem(z + (NZ - h if d == 0 else h), NZ)

    def ring(u, d, h):
        blk = x_buf.at[u, pl.ds(2 * came(d, h - 1), 2)]
        return send(
            blk, blk, ring_s, ring_r.at[u, d, h - 1],
            at(dz=1 if d == 0 else NZ - 1),
        )

    def landed(u, d, h):
        blk = x_buf.at[u, pl.ds(2 * came(d, h), 2)]
        send(
            blk, blk, ring_s, ring_r.at[u, d, h - 1],
            at(dz=1 if d == 0 else NZ - 1),
        ).wait_recv()

    def hop(u, h):
        if h == 0:
            own_half[u].wait()
            swap[u].wait_recv()
        for d in range(2):
            if 0 < h <= HOPS[u % 2][d]:
                landed(u, d, h)
            if h < HOPS[u % 2][d]:
                cp = ring(u, d, h + 1)
                cp.start()

    steps = sorted((u * STEP + h * HOP, u, h) for u in range(RING) for h in range(5))
    steps = [(u, h) for _, u, h in steps]
    hop(*steps[0])

    for i, (dz, dc) in enumerate(zc):
        cp = send(meta, mb.at[2 * z + c], meta_s, meta_r, at(dz=dz, dc=dc))
        cp.start()
    for u in range(2, RING):
        swap[u].start()

    own_half[RING].wait()
    swap[RING].wait_recv()
    for i in range(1, NX):
        cp = send(x_buf.at[RING, pl.ds(2 * z, 2)], g2_buf.at[pl.ds(2 * x, 2)], h_s, h_r, at(dx=i))
        cp.start()
    xc = [(dx, dc) for dx, dc in REL if dx]
    for i, (dx, dc) in enumerate(xc):
        cp = send(meta, mb2.at[2 * x + c], h2_s, h2_r, at(dx=dx, dc=dc))
        cp.start()
    g2_buf[pl.ds(2 * x, 2)] = x_buf[RING, pl.ds(2 * z, 2)]

    lane_row = iota((TOK, TOK), 0)
    expert = 2 * lax.rem(lane_row, 64) + lane_row // 64
    named = jnp.zeros((EXP, TOK), F32)
    gate = jnp.zeros((EXP, TOK), F32)
    for k in range(TOP):
        hit = ids_own[k : k + 1, :] == expert
        named = jnp.where(hit, 1.0, named)
        gate = jnp.where(hit, gates_own[k : k + 1, :], gate)
    before = dot(named.astype(BF), earlier())
    own_slot[...] = jnp.where(named > 0, before, 99.0)
    own_gate[...] = gate

    li_cp = []
    for i, (dy, dc) in enumerate(yc):
        g = 2 * lax.rem(y + dy, NY) + lax.rem(c + dc, 2)
        cp = send(
            li.at[:, pl.ds(pl.multiple_of(g * WID, WID), WID)], lib.at[2 * y + c],
            li_s, li_r, at(dy=dy, dc=dc),
        )
        li_cp.append(cp)

    def tables():
        bulk(mb, 15, meta_r)
        row = iota((16, TOK), 0)
        here = (row // 4) * 32 + z * 4 + lax.rem(row, 4)
        for j in range(16):
            ids = mb[j, 0:TOP, :].astype(F32).astype(jnp.int32)
            gts = mb[j, TOP:, :].astype(F32)
            nm = jnp.zeros((16, TOK), F32)
            gt = jnp.zeros((16, TOK), F32)
            for k in range(TOP):
                hit = ids[k : k + 1, :] == here
                nm = jnp.where(hit, 1.0, nm)
                gt = jnp.where(hit, gts[k : k + 1, :], gt)
            m_buf[j * 16 : (j + 1) * 16, :] = nm
            gates[j * 16 : (j + 1) * 16, :] = gt
        bef = dot(m_buf[...].astype(BF), earlier())
        slots[...] = jnp.where(m_buf[...] > 0, bef, 99.0)

        def one(j, carry):
            base = pl.multiple_of(j * 16, 16)
            sl = slots[pl.ds(base, 16), :]
            gt = gates[pl.ds(base, 16), :]
            for s in range(CAP):
                w_buf[j, s * 16 : (s + 1) * 16, :] = jnp.where(sl == float(s), gt, 0.0).astype(BF)
            return carry

        lax.fori_loop(0, 16, one, 0)

    def block(u, zb):
        for i in range(2):
            j = 2 * zb + i
            got = dot(w_buf[j], x_buf[u, j])
            for s in range(CAP):
                f_buf[u % 4, pl.ds(s * 16 + j, 16, stride=CAP * 16), :] = got[s * 16 : (s + 1) * 16, :]

    def place(u, xs, cs):
        cols = pl.ds(pl.multiple_of(cs * 1024 + u * UW, UW), UW)
        return r_buf.at[:, pl.ds(pl.multiple_of(xs * 16, 16), 16), cols]

    out_cp = []

    def rows(u, a):
        dx, dc = REL[a]
        xd, cd = lax.rem(x + dx, NX), lax.rem(c + dc, 2)
        base = pl.multiple_of((xd * 2 + cd) * (ROWS * 16), 32)
        o_buf[u, a] = f_buf[u % 4, pl.ds(base, ROWS * 16), :].astype(BF).reshape(ROWS, 16, UW)
        if a < 7:
            cp = send(o_buf.at[u, a], place(u, x, c), x_s, x_r.at[u], at(dx=dx, dc=dc))
        else:
            cp = pltpu.make_async_copy(o_buf.at[u, a], place(u, x, c), loc.at[15 + u])
            out_cp.append(cp)
        cp.start()

    def across():
        bulk(g2_buf, 6, h_r)
        bulk(mb2, 6, h2_r)
        mb2[pl.ds(2 * x, 2)] = mb[pl.ds(2 * z, 2)]
        here = x * 32 + iota((32, TOK), 0)
        for j in range(8):
            ids = mb2[j, 0:TOP, :].astype(F32).astype(jnp.int32)
            gts = mb2[j, TOP:, :].astype(F32)
            nm = jnp.zeros((32, TOK), F32)
            gt = jnp.zeros((32, TOK), F32)
            for k in range(TOP):
                hit = ids[k : k + 1, :] == here
                nm = jnp.where(hit, 1.0, nm)
                gt = jnp.where(hit, gts[k : k + 1, :], gt)
            m_buf[j * 32 : (j + 1) * 32, :] = nm
            gates[j * 32 : (j + 1) * 32, :] = gt
        bef = dot(m_buf[...].astype(BF), earlier())
        slots[...] = jnp.where(m_buf[...] > 0, bef, 99.0)
        for j in range(8):
            sl = slots[j * 32 : (j + 1) * 32, :]
            gt = gates[j * 32 : (j + 1) * 32, :]
            for s in range(CAP):
                w2_buf[j, s * 32 : (s + 1) * 32, :] = jnp.where(sl == float(s), gt, 0.0).astype(BF)
        for j in range(8):
            got = dot(w2_buf[j], g2_buf[j])
            for s in range(CAP):
                f2_buf[pl.ds(s * 8 + j, 32, stride=CAP * 8), :] = got[s * 32 : (s + 1) * 32, :]
        o2_buf[...] = f2_buf[...].astype(BF).reshape(16, ROWS * 8, UW)
        h_in[pl.ds(2 * z + c, 1)] = o2_buf[pl.ds(2 * z + c, 1)]
        to, fr = iota((128, 128), 0), iota((128, 128), 1)
        q = lax.rem(to, 64)
        want = (lax.rem(q, 16) // 2) * 16 + (to // 64) * 8 + (q // 16) * 2 + lax.rem(q, 2)
        turn[...] = (fr == want).astype(BF)
        order[...] = (2 * lax.rem(to, 64) + to // 64 == fr).astype(BF)

    h3_cp = []

    def across_send(n):
        for _ in range(n):
            i = len(h3_cp)
            if i == len(zc):
                return
            dz, dc = ACROSS[i]
            to = 2 * lax.rem(z + dz, NZ) + lax.rem(c + dc, 2)
            cp = send(o2_buf.at[to], h_in.at[2 * z + c], h3_s, h3_r, at(dz=dz, dc=dc))
            cp.start()
            h3_cp.append(cp)

    def across_done():
        bulk(h_in, 15, h3_r)
        for t in range(CAP):
            tile = pl.ds(t * 16, 16)
            both = [
                jnp.concatenate([h_in[2 * k + h, tile, :] for k in range(NZ)], axis=0) for h in range(2)
            ]
            got = dot(turn[...], jnp.concatenate(both, axis=1)).astype(BF)
            for h in range(2):
                col = h * 1024 + RING * UW
                r_buf[2 * t : 2 * t + 2, :, col : col + UW] = got[:, h * UW : (h + 1) * UW].reshape(2, 64, UW)

    def work(u, h):
        if h == 0:
            block(u, z)
        for d in range(2):
            if 0 < h <= HOPS[u % 2][d]:
                block(u, came(d, h))
        if h == 4:
            for a in range(8):
                rows(u, a)
            if u == 1:
                across()
            across_send(SPREAD[u])

    late = [steps[0]]
    for n, (u, h) in enumerate(steps[1:]):
        hop(u, h)
        late.append((u, h))
        if n == 2:
            for cp in li_cp:
                cp.start()
            tables()
        if n >= 2:
            for q in late:
                work(*q)
            late = []

    own_li.wait()
    bulk(lib, 7, li_r)
    eye = (iota((TOK, TOK), 0) == iota((TOK, TOK), 1)).astype(BF)
    for g in range(8):
        lit[:, g * TOK : (g + 1) * TOK] = dot(lib[g], eye, ((0,), (0,))).astype(BF)

    load_e.wait()
    for u in ORDER:
        if u == RING:
            across_done()
        else:
            taken(o_buf.at[u, pl.ds(0, 7)], x_r.at[u])
            out_cp[u].wait()
        for h in range(2):
            cols = pl.ds(h * 1024 + u * UW, UW)
            cp = pltpu.make_async_copy(r_buf.at[:, :, cols], grows.at[:, :, cols], loc.at[0])
            cp.start()

        def score(r, carry, u=u):
            tot = jnp.zeros((64, 128), F32)
            for h in range(2):
                col = h * 1024 + u * UW
                a = r_buf[r, :, col : col + 128].astype(F32)
                b = e_buf[r, :, col : col + 128].astype(F32)
                tot = tot + a * b
            acc[r] = tot if u == 0 else acc[r] + tot
            return carry

        lax.fori_loop(0, ROWS, score, 0)

    total = jnp.zeros((64, 128), F32)
    for r in range(ROWS):
        total = jnp.where(iota((64, 128), 1) == r, jnp.sum(acc[r], axis=1, keepdims=True), total)
    s_out[...] = total.reshape(64, 1, 128)

    def sc(i):
        to = lax.rem(idx + i, 64)
        return send(s_out.at[to], t_in.at[idx], sc_s, sc_r, (y, to))

    def sc_start(i, carry):
        sc(i).start()
        return carry

    lax.fori_loop(1, 64, sc_start, 0)
    t_in[pl.ds(idx, 1)] = s_out[pl.ds(idx, 1)]
    taken(x_buf.at[:, 0], xch_s)
    taken(x_buf.at[pl.ds(0, RING), pl.ds(0, 14)], ring_s)
    taken(o_buf.at[pl.ds(0, RING), pl.ds(0, 7)], x_s)
    bulk(mb, 15, meta_s)
    bulk(lib, 7, li_s)
    bulk(g2_buf, 6, h_s)
    bulk(mb2, 6, h2_s)
    bulk(h_in, 15, h3_s)
    bulk(t_in, 63, sc_r)

    back = t_in[...].reshape(64, 128)
    scaled = []
    for l in range(2):
        sl = own_slot[l * 64 : (l + 1) * 64, :]
        v = jnp.zeros((64, TOK), F32)
        for s in range(CAP):
            v = jnp.where(sl == float(s), back[:, l * CAP + s : l * CAP + s + 1], v)
        scaled.append(v)
    scaled = jnp.concatenate(scaled, axis=0)
    logits = scaled - own_gate[...] * jnp.sum(scaled, axis=0, keepdims=True)
    glt[...] = dot(logits.astype(BF), order[...], ((0,), (0,))).astype(BF)

    for i, (dy, dc) in enumerate(yc):
        cp = send(glt, glb.at[2 * y + c], gl_s, gl_r, at(dy=dy, dc=dc))
        cp.start()
    glb[pl.ds(2 * y + c, 1)] = glt[...].reshape(1, TOK, EXP)
    load_rw.wait()
    gin[...] = dot(glt[...], rw[...], ((1,), (1,))).astype(BF)
    cp = pltpu.make_async_copy(gin, gin_out, loc.at[1])
    cp.start()
    bulk(glb, 7, gl_r)
    part[...] = dot(lit[...], glb[...].reshape(8 * TOK, EXP))

    chip = x * NZ + z

    def chip_at(i):
        q = lax.rem(chip + i, 32)
        return q, (y, q * 2 + c)

    def rs_start(i, carry):
        q, to = chip_at(i)
        send(
            part.at[pl.ds(pl.multiple_of(q * 8, 8), 8)], rb.at[chip], rs_s, rs_r, to
        ).start()
        return carry

    lax.fori_loop(1, 32, rs_start, 0)
    rb[pl.ds(chip, 1)] = part[pl.ds(pl.multiple_of(chip * 8, 8), 8), :].reshape(1, 8, EXP)
    bulk(s_out, 63, sc_s)
    bulk(glb, 7, gl_s)
    bulk(rb, 31, rs_r)
    fin[...] = jnp.sum(rb[...], axis=0)

    def a1_start(i, carry):
        q, to = chip_at(i)
        send(fin, ag.at[chip], a1_s, a1_r, to).start()
        return carry

    lax.fori_loop(1, 32, a1_start, 0)
    ag[pl.ds(chip, 1)] = fin[...].reshape(1, 8, EXP)
    bulk(rb, 31, rs_s)
    bulk(ag, 31, a1_r)
    half[...] = ag[...].reshape(256, EXP).astype(BF)

    for i in range(1, NY):
        cp = send(half, agb.at[2 * y + c], a2_s, a2_r.at[i], at(dy=i))
        cp.start()

    def swap_part(g, src):
        send(src, agb.at[g], a3_s, a3_r, at(dc=1)).start()

    swap_part(2 * y + c, half)
    agb[pl.ds(2 * y + c, 1)] = half[...].reshape(1, 256, EXP)
    bulk(ag, 31, a1_s)
    taken(r_buf, loc.at[0])
    taken(gin, loc.at[1])
    for i in range(1, NY):
        ys = lax.rem(y + NY - i, NY)
        send(half, agb.at[2 * ys + c], a2_s, a2_r.at[i], at(dy=i)).wait_recv()
        swap_part(2 * ys + c, agb.at[2 * ys + c])
    bulk(agb, NY, a3_r)
    store = pltpu.make_async_copy(agb, agb_out, loc.at[0])
    store.start()
    bulk(agb, NY - 1, a2_s)
    bulk(agb, NY, a3_s)
    store.wait()


def writer(rows_in, gin_in, agb_in, grows, gin_out, grout, rows, gin, parts, wide, loc, sto):
    pieces = [pl.ds(3 * i, 3) for i in range(6)]
    loads = [pltpu.make_async_copy(agb_in, parts, loc.at[6]), pltpu.make_async_copy(gin_in, gin, loc.at[7])]
    loads += [pltpu.make_async_copy(rows_in.at[p], rows.at[p], loc.at[i]) for i, p in enumerate(pieces)]
    for cp in loads:
        cp.start()
    loads[0].wait()
    wide[...] = parts[...].reshape(D, EXP).astype(F32)
    pltpu.make_async_copy(wide, grout, sto.at[0]).start()
    loads[1].wait()
    pltpu.make_async_copy(gin, gin_out, sto.at[1]).start()
    for i, p in enumerate(pieces):
        loads[2 + i].wait()
        pltpu.make_async_copy(rows.at[p], grows.at[p], sto.at[2]).start()
    pltpu.make_async_copy(wide, grout, sto.at[0]).wait()
    pltpu.make_async_copy(gin, gin_out, sto.at[1]).wait()
    pltpu.make_async_copy(rows, grows, sto.at[2]).wait()


def body(grad_out, layer_input, router_weight, gate_probs, expert_ids, expert_out):
    eo = expert_out[0].transpose(0, 2, 1, 3).reshape(ROWS, 64, D)
    vm, sem = pltpu.VMEM, pltpu.SemaphoreType.DMA
    hbm = pl.BlockSpec(memory_space=pltpu.HBM)
    results = pl.pallas_call(
        kernel,
        out_shape=(
            jax.ShapeDtypeStruct((ROWS, 64, D), BF),
            jax.ShapeDtypeStruct((TOK, D), BF),
            jax.ShapeDtypeStruct((8, 256, EXP), BF),
        ),
        in_specs=[hbm] * 6,
        out_specs=(hbm, hbm, hbm),
        scratch_shapes=[
            vm((UNITS, 16, TOK, UW), BF),
            vm((4, 8 * ROWS * 16, UW), F32),
            vm((UNITS, 8, ROWS, 16, UW), BF),
            vm((16, CAP * 16, TOK), BF),
            vm((ROWS, 64, D), BF),
            vm((TOK, D), BF),
            vm((8, 256, EXP), BF),
            vm((ROWS, 64, D), BF),
            vm((D, EXP), BF),
            vm((TOP, TOK), jnp.int32),
            vm((TOP, TOK), F32),
            vm((2 * TOP, TOK), BF),
            vm((16, 2 * TOP, TOK), BF),
            vm((256, TOK), F32),
            vm((256, TOK), F32),
            vm((256, TOK), F32),
            vm((8, 2 * TOP, TOK), BF),
            vm((8, TOK, UW), BF),
            vm((8, CAP * 32, TOK), BF),
            vm((16 * ROWS * 8, UW), F32),
            vm((16, ROWS * 8, UW), BF),
            vm((16, ROWS * 8, UW), BF),
            vm((128, 128), BF),
            vm((128, 128), BF),
            vm((EXP, TOK), F32),
            vm((EXP, TOK), F32),
            vm((ROWS, 64, 128), F32),
            vm((64, 1, 128), F32),
            vm((64, 1, 128), F32),
            vm((8, TOK, WID), BF),
            vm((WID, 8 * TOK), BF),
            vm((TOK, EXP), BF),
            vm((8, TOK, EXP), BF),
            vm((WID, EXP), F32),
            vm((32, 8, EXP), F32),
            vm((8, EXP), F32),
            vm((32, 8, EXP), F32),
            vm((256, EXP), BF),
            sem((22,)),
            sem, sem((UNITS,)),
            sem, sem((RING, 2, 4)),
            sem, sem,
            sem, sem,
            sem, sem((RING,)),
            sem, sem, sem, sem, sem, sem,
            sem, sem,
            sem, sem,
            sem, sem,
            sem, sem,
            sem, sem((NY,)),
            sem, sem,
        ],
        compiler_params=pltpu.CompilerParams(
            collective_id=0, has_side_effects=True, vmem_limit_bytes=57 * 2**20
        ),
    )(grad_out, layer_input, router_weight, expert_ids.T, gate_probs.T, eo)
    grows, gin, grout = pl.pallas_call(
        writer,
        out_shape=(
            jax.ShapeDtypeStruct((ROWS, 64, D), BF),
            jax.ShapeDtypeStruct((TOK, D), BF),
            jax.ShapeDtypeStruct((D, EXP), F32),
        ),
        in_specs=[hbm] * 3,
        out_specs=(hbm, hbm, hbm),
        scratch_shapes=[
            vm((ROWS, 64, D), BF), vm((TOK, D), BF), vm((8, 256, EXP), BF), vm((D, EXP), F32),
            sem((8,)), sem((3,)),
        ],
        compiler_params=pltpu.CompilerParams(vmem_limit_bytes=57 * 2**20),
    )(*results)
    grows = grows.reshape(2, CAP, 64, D).transpose(0, 2, 1, 3)
    return grows[None], gin, grout


def solution(mesh):
    return jax.shard_map(
        body,
        mesh=mesh,
        in_specs=(
            P(("dp", "expert"), None),
            P(("dp", "expert"), None),
            P(),
            P(("dp", "expert"), None),
            P(("dp", "expert"), None),
            P("dp", "expert", None, None, None),
        ),
        out_specs=(P("dp", "expert", None, None, None), P(("dp", "expert"), None), P()),
        check_vma=False,
    )
```

```python
import jax
import jax.numpy as jnp
from jax import lax
from jax.experimental import pallas as pl
from jax.experimental.pallas import tpu as pltpu
from jax.sharding import PartitionSpec as P

MESH = pl.DeviceIdType.MESH
BF, F32 = jnp.bfloat16, jnp.float32
NX, NZ, NY = 4, 8, 4
D, TOK, TOP, EXP, CAP = 2048, 128, 8, 128, 9
ROWS = 2 * CAP
UNITS, UW, WID = 8, 128, 256
RING = 7
HOPS = ((4, 3), (3, 4))
STEP, HOP = 4.8, 3.3
ORDER = (0, 1, 2, 3, 4, 5, 7, 6)
ACROSS = tuple((dz, dc) for dz in (4, 3, 5, 2, 6, 1, 7) for dc in range(2)) + ((0, 1),)
SPREAD = {(5, 4): 2, (6, 3): 13}
REL = ((2, 0), (2, 1), (1, 0), (3, 0), (1, 1), (3, 1), (0, 1), (0, 0))


def iota(shape, axis):
    return lax.broadcasted_iota(jnp.int32, shape, axis)


def dot(a, b, dims=((1,), (0,))):
    return lax.dot_general(a, b, (dims, ((), ())), preferred_element_type=F32)


def earlier():
    return (iota((TOK, TOK), 0) < iota((TOK, TOK), 1)).astype(BF)


def kernel(
    go, li, rw_in, ids_in, gates_in, eo, grows, gin_out, agb_out,
    x_buf, f_buf, o_buf, w_buf, r_buf, gin, agb, e_buf, rw, ids_own, gates_own, meta, mb, slots, gates, m_buf, mb2, g2_buf, w2_buf, f2_buf, o2_buf, h_in, turn, mb3, few, fews,
    own_slot, own_gate, acc, s_out, t_in, count, lib, lit, glt, glb, part, rb, fin, ag, half,
    loc, xch_s, xch_r, ring_s, ring_r, meta_s, meta_r, li_s, li_r, x_s, x_r, h_s, h_r, h2_s, h2_r, h3_s, h3_r, h4_s, h4_r,
    sc_s, sc_r, gl_s, gl_r, rs_s, rs_r, a1_s, a1_r, a2_s, a2_r, a3_s, a3_r,
):
    y = lax.axis_index("dp")
    idx = lax.axis_index("expert")
    x, z, c = idx // 16, (idx // 2) % NZ, idx % 2

    def at(dx=0, dy=0, dz=0, dc=0):
        xx, zz, cc = lax.rem(x + dx, NX), lax.rem(z + dz, NZ), lax.rem(c + dc, 2)
        return (lax.rem(y + dy, NY), xx * 16 + zz * 2 + cc)

    def bulk(ref, n, s):
        pltpu.make_async_copy(ref.at[pl.ds(0, n)], ref.at[pl.ds(0, n)], s).wait()

    def taken(ref, s):
        pltpu.make_async_copy(ref, ref, s).wait()

    def send(src, dst, ss, rs, to):
        return pltpu.make_async_remote_copy(
            src_ref=src, dst_ref=dst, send_sem=ss, recv_sem=rs, device_id=to, device_id_type=MESH
        )

    load_ids = pltpu.make_async_copy(ids_in, ids_own, loc.at[6])
    load_ids.start()
    load_gates = pltpu.make_async_copy(gates_in, gates_own, loc.at[2])
    load_gates.start()
    load_e = pltpu.make_async_copy(eo, e_buf, loc.at[0])
    load_e.start()
    own_half = []
    for u in range(UNITS):
        cols = pl.ds(pl.multiple_of(c * 1024 + u * UW, UW), UW)
        cp = pltpu.make_async_copy(go.at[:, cols], x_buf.at[u, 2 * z + c], loc.at[7 + u])
        cp.start()
        own_half.append(cp)
    own_li = pltpu.make_async_copy(
        li.at[:, pl.ds(pl.multiple_of((2 * y + c) * WID, WID), WID)], lib.at[2 * y + c], loc.at[5]
    )
    own_li.start()
    load_rw = pltpu.make_async_copy(rw_in, rw, loc.at[3])
    load_rw.start()

    barrier = pltpu.get_barrier_semaphore()
    zc = [(dz, dc) for dz in range(NZ) for dc in range(2) if dz or dc]
    yc = [(dy, dc) for dy in range(NY) for dc in range(2) if dy or dc]
    greet = [dict(dz=a, dc=b) for a, b in zc]
    greet += [dict(dx=a, dc=b) for a, b in REL if a]
    greet += [dict(dy=a, dc=b) for a, b in yc if a]
    for g in greet:
        pl.semaphore_signal(barrier, inc=1, device_id=at(**g), device_id_type=MESH)
    load_ids.wait()
    load_gates.wait()
    meta[0:TOP, :] = ids_own[...].astype(F32).astype(BF)
    meta[TOP:, :] = gates_own[...].astype(BF)
    mb[pl.ds(2 * z + c, 1)] = meta[...].reshape(1, 2 * TOP, TOK)
    pl.semaphore_wait(barrier, len(greet))


    swap = []
    for u in range(UNITS):
        cols = pl.ds(pl.multiple_of((1 - c) * 1024 + u * UW, UW), UW)
        swap.append(
            send(go.at[:, cols], x_buf.at[u, 2 * z + c], xch_s, xch_r.at[u], at(dc=1))
        )
    swap[0].start()
    swap[RING].start()
    swap[1].start()

    def came(d, h):
        return lax.rem(z + (NZ - h if d == 0 else h), NZ)

    def ring(u, d, h):
        blk = x_buf.at[u, pl.ds(2 * came(d, h - 1), 2)]
        return send(
            blk, blk, ring_s, ring_r.at[u, d, h - 1],
            at(dz=1 if d == 0 else NZ - 1),
        )

    def landed(u, d, h):
        blk = x_buf.at[u, pl.ds(2 * came(d, h), 2)]
        send(
            blk, blk, ring_s, ring_r.at[u, d, h - 1],
            at(dz=1 if d == 0 else NZ - 1),
        ).wait_recv()

    def ring0(d, h, i):
        blk = x_buf.at[0, pl.ds(2 * came(d, h - 1) + (c if i == 0 else 1 - c), 1)]
        return send(
            blk, blk, ring_s, ring_r.at[RING * i, d, h - 1], at(dz=1 if d == 0 else NZ - 1)
        )

    def landed0(d, h, i):
        blk = x_buf.at[0, pl.ds(2 * came(d, h) + (c if i == 0 else 1 - c), 1)]
        send(
            blk, blk, ring_s, ring_r.at[RING * i, d, h - 1], at(dz=1 if d == 0 else NZ - 1)
        ).wait_recv()

    def hop0(h):
        for i in range(2):
            if h == 0 and i == 0:
                own_half[0].wait()
            if h == 0 and i == 1:
                swap[0].wait_recv()
            for d in range(2):
                if 0 < h <= HOPS[0][d]:
                    landed0(d, h, i)
                if h < HOPS[0][d]:
                    ring0(d, h + 1, i).start()

    def hop(u, h):
        if u == 0:
            hop0(h)
            return
        if h == 0:
            own_half[u].wait()
            swap[u].wait_recv()
        for d in range(2):
            if 0 < h <= HOPS[u % 2][d]:
                landed(u, d, h)
            if h < HOPS[u % 2][d]:
                cp = ring(u, d, h + 1)
                cp.start()

    steps = sorted((u * STEP + h * HOP, u, h) for u in range(RING) for h in range(5))
    steps = [(u, h) for _, u, h in steps]
    hop(*steps[0])

    for i, (dz, dc) in enumerate(zc):
        cp = send(meta, mb.at[2 * z + c], meta_s, meta_r, at(dz=dz, dc=dc))
        cp.start()
    for u in range(2, RING):
        swap[u].start()
    for dy, dc in yc:
        send(meta, mb3.at[2 * y + c], h4_s, h4_r, at(dy=dy, dc=dc)).start()
    mb3[pl.ds(2 * y + c, 1)] = meta[...].reshape(1, 2 * TOP, TOK)

    own_half[RING].wait()
    swap[RING].wait_recv()
    for i in range(1, NX):
        cp = send(x_buf.at[RING, pl.ds(2 * z, 2)], g2_buf.at[pl.ds(2 * x, 2)], h_s, h_r, at(dx=i))
        cp.start()
    xc = [(dx, dc) for dx, dc in REL if dx]
    for i, (dx, dc) in enumerate(xc):
        cp = send(meta, mb2.at[2 * x + c], h2_s, h2_r, at(dx=dx, dc=dc))
        cp.start()
    g2_buf[pl.ds(2 * x, 2)] = x_buf[RING, pl.ds(2 * z, 2)]

    lane_row = iota((TOK, TOK), 0)
    expert = 2 * lax.rem(lane_row, 64) + lane_row // 64
    named = jnp.zeros((EXP, TOK), F32)
    gate = jnp.zeros((EXP, TOK), F32)
    for k in range(TOP):
        hit = ids_own[k : k + 1, :] == expert
        named = jnp.where(hit, 1.0, named)
        gate = jnp.where(hit, gates_own[k : k + 1, :], gate)
    before = dot(named.astype(BF), earlier())
    own_slot[...] = jnp.where(named > 0, before, 99.0)
    own_gate[...] = gate

    li_cp = []
    for i, (dy, dc) in enumerate(yc):
        g = 2 * lax.rem(y + dy, NY) + lax.rem(c + dc, 2)
        cp = send(
            li.at[:, pl.ds(pl.multiple_of(g * WID, WID), WID)], lib.at[2 * y + c],
            li_s, li_r, at(dy=dy, dc=dc),
        )
        li_cp.append(cp)

    def tables():
        bulk(mb, 15, meta_r)
        row = iota((16, TOK), 0)
        here = (row // 4) * 32 + z * 4 + lax.rem(row, 4)
        for j in range(16):
            ids = mb[j, 0:TOP, :].astype(F32).astype(jnp.int32)
            gts = mb[j, TOP:, :].astype(F32)
            nm = jnp.zeros((16, TOK), F32)
            gt = jnp.zeros((16, TOK), F32)
            for k in range(TOP):
                hit = ids[k : k + 1, :] == here
                nm = jnp.where(hit, 1.0, nm)
                gt = jnp.where(hit, gts[k : k + 1, :], gt)
            m_buf[j * 16 : (j + 1) * 16, :] = nm
            gates[j * 16 : (j + 1) * 16, :] = gt
        bef = dot(m_buf[...].astype(BF), earlier())
        slots[...] = jnp.where(m_buf[...] > 0, bef, 99.0)

        def one(j, carry):
            base = pl.multiple_of(j * 16, 16)
            sl = slots[pl.ds(base, 16), :]
            gt = gates[pl.ds(base, 16), :]
            for s in range(CAP):
                w_buf[j, s * 16 : (s + 1) * 16, :] = jnp.where(sl == float(s), gt, 0.0).astype(BF)
            return carry

        lax.fori_loop(0, 16, one, 0)

    def block(u, zb):
        for i in range(2):
            j = 2 * zb + i
            got = dot(w_buf[j], x_buf[u, j])
            for s in range(CAP):
                f_buf[u % 4, pl.ds(s * 16 + j, 16, stride=CAP * 16), :] = got[s * 16 : (s + 1) * 16, :]

    def place(u, xs, cs):
        cols = pl.ds(pl.multiple_of(cs * 1024 + u * UW, UW), UW)
        return r_buf.at[:, pl.ds(pl.multiple_of(xs * 16, 16), 16), cols]

    out_cp = []

    def rows(u, a):
        dx, dc = REL[a]
        xd, cd = lax.rem(x + dx, NX), lax.rem(c + dc, 2)
        base = pl.multiple_of((xd * 2 + cd) * (ROWS * 16), 32)
        o_buf[u, a] = f_buf[u % 4, pl.ds(base, ROWS * 16), :].astype(BF).reshape(ROWS, 16, UW)
        if a < 7:
            cp = send(o_buf.at[u, a], place(u, x, c), x_s, x_r.at[u], at(dx=dx, dc=dc))
        else:
            cp = pltpu.make_async_copy(o_buf.at[u, a], place(u, x, c), loc.at[15 + u])
            out_cp.append(cp)
        cp.start()

    def across():
        bulk(g2_buf, 6, h_r)
        bulk(mb2, 6, h2_r)
        mb2[pl.ds(2 * x, 2)] = mb[pl.ds(2 * z, 2)]
        here = x * 32 + iota((32, TOK), 0)
        for j in range(8):
            ids = mb2[j, 0:TOP, :].astype(F32).astype(jnp.int32)
            gts = mb2[j, TOP:, :].astype(F32)
            nm = jnp.zeros((32, TOK), F32)
            gt = jnp.zeros((32, TOK), F32)
            for k in range(TOP):
                hit = ids[k : k + 1, :] == here
                nm = jnp.where(hit, 1.0, nm)
                gt = jnp.where(hit, gts[k : k + 1, :], gt)
            m_buf[j * 32 : (j + 1) * 32, :] = nm
            gates[j * 32 : (j + 1) * 32, :] = gt
        bef = dot(m_buf[...].astype(BF), earlier())
        slots[...] = jnp.where(m_buf[...] > 0, bef, 99.0)
        for j in range(8):
            sl = slots[j * 32 : (j + 1) * 32, :]
            gt = gates[j * 32 : (j + 1) * 32, :]
            for s in range(CAP):
                w2_buf[j, s * 32 : (s + 1) * 32, :] = jnp.where(sl == float(s), gt, 0.0).astype(BF)
        for j in range(8):
            got = dot(w2_buf[j], g2_buf[j])
            for s in range(CAP):
                f2_buf[pl.ds(s * 8 + j, 32, stride=CAP * 8), :] = got[s * 32 : (s + 1) * 32, :]
        o2_buf[...] = f2_buf[...].astype(BF).reshape(16, ROWS * 8, UW)
        h_in[pl.ds(2 * z + c, 1)] = o2_buf[pl.ds(2 * z + c, 1)]
        to, fr = iota((128, 128), 0), iota((128, 128), 1)
        q = lax.rem(to, 64)
        want = (lax.rem(q, 16) // 2) * 16 + (to // 64) * 8 + (q // 16) * 2 + lax.rem(q, 2)
        turn[...] = (fr == want).astype(BF)

    h3_cp = []

    def across_send(n):
        for _ in range(n):
            i = len(h3_cp)
            if i == len(zc):
                return
            dz, dc = ACROSS[i]
            to = 2 * lax.rem(z + dz, NZ) + lax.rem(c + dc, 2)
            cp = send(o2_buf.at[to], h_in.at[2 * z + c], h3_s, h3_r, at(dz=dz, dc=dc))
            cp.start()
            h3_cp.append(cp)

    def across_done():
        bulk(h_in, 15, h3_r)
        for t in range(CAP):
            tile = pl.ds(t * 16, 16)
            both = [
                jnp.concatenate([h_in[2 * k + h, tile, :] for k in range(NZ)], axis=0) for h in range(2)
            ]
            got = dot(turn[...], jnp.concatenate(both, axis=1)).astype(BF)
            for h in range(2):
                col = h * 1024 + RING * UW
                r_buf[2 * t : 2 * t + 2, :, col : col + UW] = got[:, h * UW : (h + 1) * UW].reshape(2, 64, UW)

    def work(u, h):
        if h == 0:
            block(u, z)
        for d in range(2):
            if 0 < h <= HOPS[u % 2][d]:
                block(u, came(d, h))
        if h == 4:
            for a in range(8):
                rows(u, a)
            if u == 1:
                across()

    late = [steps[0]]
    for n, (u, h) in enumerate(steps[1:]):
        hop(u, h)
        late.append((u, h))
        across_send(SPREAD.get((u, h), 0))
        if n == 2:
            for cp in li_cp:
                cp.start()
            tables()
        if n >= 2:
            for q in late:
                work(*q)
            late = []

    own_li.wait()
    bulk(lib, 7, li_r)
    eye = (iota((TOK, TOK), 0) == iota((TOK, TOK), 1)).astype(BF)
    for g in range(8):
        lit[:, g * TOK : (g + 1) * TOK] = dot(lib[g], eye, ((0,), (0,))).astype(BF)

    load_e.wait()
    for u in ORDER:
        if u == RING:
            across_done()
        else:
            taken(o_buf.at[u, pl.ds(0, 7)], x_r.at[u])
            out_cp[u].wait()
        for h in range(2):
            cols = pl.ds(h * 1024 + u * UW, UW)
            cp = pltpu.make_async_copy(r_buf.at[:, :, cols], grows.at[:, :, cols], loc.at[0])
            cp.start()

        def score(r, carry, u=u):
            tot = jnp.zeros((64, 128), F32)
            for h in range(2):
                col = h * 1024 + u * UW
                a = r_buf[r, :, col : col + 128].astype(F32)
                b = e_buf[r, :, col : col + 128].astype(F32)
                tot = tot + a * b
            acc[r] = tot if u == 0 else acc[r] + tot
            return carry

        lax.fori_loop(0, ROWS, score, 0)

    total = jnp.zeros((64, 128), F32)
    for r in range(ROWS):
        total = jnp.where(iota((64, 128), 1) == r, jnp.sum(acc[r], axis=1, keepdims=True), total)
    s_out[...] = total

    def sc(i):
        to = lax.rem(idx + i, 64)
        return send(s_out.at[pl.ds(to, 1)], t_in.at[pl.ds(idx, 1)], sc_s, sc_r, (y, to))

    def sc_start(i, carry):
        sc(i).start()
        return carry

    lax.fori_loop(1, 64, sc_start, 0)
    t_in[pl.ds(idx, 1)] = s_out[pl.ds(idx, 1)]
    taken(x_buf.at[:, 0], xch_s)
    taken(x_buf.at[pl.ds(0, RING), pl.ds(0, 14)], ring_s)
    taken(o_buf.at[pl.ds(0, RING), pl.ds(0, 7)], x_s)
    bulk(mb, 15, meta_s)
    bulk(lib, 7, li_s)
    bulk(g2_buf, 6, h_s)
    bulk(mb2, 6, h2_s)
    bulk(h_in, 15, h3_s)
    bulk(mb3, 7, h4_s)
    bulk(mb3, 7, h4_r)
    taken(count, sc_r)

    back = t_in[...]
    scaled = []
    for l in range(2):
        sl = own_slot[l * 64 : (l + 1) * 64, :]
        v = jnp.zeros((64, TOK), F32)
        for s in range(CAP):
            v = jnp.where(sl == float(s), back[:, l * CAP + s : l * CAP + s + 1], v)
        scaled.append(v)
    scaled = jnp.concatenate(scaled, axis=0)
    total = jnp.sum(scaled, axis=0, keepdims=True)
    for k in range(TOP):
        mine = jnp.sum(jnp.where(ids_own[k : k + 1, :] == expert, scaled, 0.0), axis=0, keepdims=True)
        few[k : k + 1, :] = mine - gates_own[k : k + 1, :] * total

    for dy, dc in yc:
        send(few, fews.at[2 * y + c], gl_s, gl_r, at(dy=dy, dc=dc)).start()
    fews[pl.ds(2 * y + c, 1)] = few[...].reshape(1, TOP, TOK)

    def spread(ids, vals):
        got = jnp.zeros((EXP, TOK), F32)
        for k in range(TOP):
            got = jnp.where(ids[k : k + 1, :] == lane_row, vals[k : k + 1, :], got)
        return got.astype(BF)

    glt[...] = spread(ids_own[...], few[...])
    load_rw.wait()
    gin[...] = dot(glt[...], rw[...], ((0,), (1,))).astype(BF)
    pltpu.make_async_copy(gin, gin_out, loc.at[1]).start()
    bulk(fews, 7, gl_r)
    for j in range(8):
        glb[:, j * TOK : (j + 1) * TOK] = spread(mb3[j, 0:TOP, :].astype(F32).astype(jnp.int32), fews[j])
    part[...] = dot(lit[...], glb[...], ((1,), (1,))).astype(BF)

    chip = x * NZ + z
    seat = x * 4 + z // 2
    owner = lax.rem(z, 2) == 0

    def seat_at(q):
        return (y, (q // 4) * 16 + lax.rem(q, 4) * 4 + c)

    def rs_start(i, carry):
        q = lax.rem(seat + i, 16)
        send(
            part.at[pl.ds(pl.multiple_of(q * 16, 16), 16)], rb.at[chip], rs_s, rs_r, seat_at(q)
        ).start()
        return carry

    def a1_start(i, carry):
        q = lax.rem(chip + i, 32)
        send(fin, ag.at[seat], a1_s, a1_r, (y, q * 2 + c)).start()
        return carry

    lax.fori_loop(1, 16, rs_start, 0)

    @pl.when(owner)
    def _():
        rb[pl.ds(chip, 1)] = part[pl.ds(pl.multiple_of(seat * 16, 16), 16), :].reshape(1, 16, EXP)
        taken(count, sc_s)
        bulk(fews, 7, gl_s)
        bulk(rb, 31, rs_r)
        fin[...] = jnp.sum(rb[...].astype(F32), axis=0).astype(BF)
        lax.fori_loop(1, 32, a1_start, 0)
        ag[pl.ds(seat, 1)] = fin[...].reshape(1, 16, EXP)
        bulk(rb, 15, rs_s)
        bulk(ag, 15, a1_r)

    @pl.when(jnp.logical_not(owner))
    def _():
        rs_start(0, 0)
        taken(count, sc_s)
        bulk(fews, 7, gl_s)
        bulk(rb, 16, rs_s)
        bulk(ag, 16, a1_r)

    half[...] = ag[...].reshape(256, EXP)

    for i in range(1, NY):
        cp = send(half, agb.at[2 * y + c], a2_s, a2_r.at[i], at(dy=i))
        cp.start()

    def swap_part(g, src):
        send(src, agb.at[g], a3_s, a3_r, at(dc=1)).start()

    swap_part(2 * y + c, half)
    agb[pl.ds(2 * y + c, 1)] = half[...].reshape(1, 256, EXP)

    @pl.when(owner)
    def _():
        bulk(rb, 31, a1_s)

    taken(r_buf, loc.at[0])
    taken(gin, loc.at[1])
    for i in range(1, NY):
        ys = lax.rem(y + NY - i, NY)
        send(half, agb.at[2 * ys + c], a2_s, a2_r.at[i], at(dy=i)).wait_recv()
        swap_part(2 * ys + c, agb.at[2 * ys + c])
    bulk(agb, NY, a3_r)
    store = pltpu.make_async_copy(agb, agb_out, loc.at[0])
    store.start()
    bulk(agb, NY - 1, a2_s)
    bulk(agb, NY, a3_s)
    store.wait()


def writer(rows_in, gin_in, agb_in, grows, gin_out, grout, rows, gin, parts, wide, loc, sto):
    pieces = [pl.ds(3 * i, 3) for i in range(6)]
    loads = [pltpu.make_async_copy(agb_in, parts, loc.at[6]), pltpu.make_async_copy(gin_in, gin, loc.at[7])]
    loads += [pltpu.make_async_copy(rows_in.at[p], rows.at[p], loc.at[i]) for i, p in enumerate(pieces)]
    for cp in loads:
        cp.start()
    loads[0].wait()
    wide[...] = parts[...].reshape(D, EXP).astype(F32)
    pltpu.make_async_copy(wide, grout, sto.at[0]).start()
    loads[1].wait()
    pltpu.make_async_copy(gin, gin_out, sto.at[1]).start()
    for i, p in enumerate(pieces):
        loads[2 + i].wait()
        pltpu.make_async_copy(rows.at[p], grows.at[p], sto.at[2]).start()
    pltpu.make_async_copy(wide, grout, sto.at[0]).wait()
    pltpu.make_async_copy(gin, gin_out, sto.at[1]).wait()
    pltpu.make_async_copy(rows, grows, sto.at[2]).wait()


def body(grad_out, layer_input, router_weight, gate_probs, expert_ids, expert_out):
    eo = expert_out[0].transpose(0, 2, 1, 3).reshape(ROWS, 64, D)
    vm, sem = pltpu.VMEM, pltpu.SemaphoreType.DMA
    hbm = pl.BlockSpec(memory_space=pltpu.HBM)
    results = pl.pallas_call(
        kernel,
        out_shape=(
            jax.ShapeDtypeStruct((ROWS, 64, D), BF),
            jax.ShapeDtypeStruct((TOK, D), BF),
            jax.ShapeDtypeStruct((8, 256, EXP), BF),
        ),
        in_specs=[hbm] * 6,
        out_specs=(hbm, hbm, hbm),
        scratch_shapes=[
            vm((UNITS, 16, TOK, UW), BF),
            vm((4, 8 * ROWS * 16, UW), F32),
            vm((UNITS, 8, ROWS, 16, UW), BF),
            vm((16, CAP * 16, TOK), BF),
            vm((ROWS, 64, D), BF),
            vm((TOK, D), BF),
            vm((8, 256, EXP), BF),
            vm((ROWS, 64, D), BF),
            vm((D, EXP), BF),
            vm((TOP, TOK), jnp.int32),
            vm((TOP, TOK), F32),
            vm((2 * TOP, TOK), BF),
            vm((16, 2 * TOP, TOK), BF),
            vm((256, TOK), F32),
            vm((256, TOK), F32),
            vm((256, TOK), F32),
            vm((8, 2 * TOP, TOK), BF),
            vm((8, TOK, UW), BF),
            vm((8, CAP * 32, TOK), BF),
            vm((16 * ROWS * 8, UW), F32),
            vm((16, ROWS * 8, UW), BF),
            vm((16, ROWS * 8, UW), BF),
            vm((128, 128), BF),
            vm((8, 2 * TOP, TOK), BF),
            vm((TOP, TOK), F32),
            vm((8, TOP, TOK), F32),
            vm((EXP, TOK), F32),
            vm((EXP, TOK), F32),
            vm((ROWS, 64, 128), F32),
            vm((64, 128), F32),
            vm((64, 128), F32),
            vm((63, 1, 128), F32),
            vm((8, TOK, WID), BF),
            vm((WID, 8 * TOK), BF),
            vm((EXP, TOK), BF),
            vm((EXP, 8 * TOK), BF),
            vm((WID, EXP), BF),
            vm((32, 16, EXP), BF),
            vm((16, EXP), BF),
            vm((16, 16, EXP), BF),
            vm((256, EXP), BF),
            sem((22,)),
            sem, sem((UNITS,)),
            sem, sem((RING + 1, 2, 4)),
            sem, sem,
            sem, sem,
            sem, sem((RING,)),
            sem, sem, sem, sem, sem, sem, sem, sem,
            sem, sem,
            sem, sem,
            sem, sem,
            sem, sem,
            sem, sem((NY,)),
            sem, sem,
        ],
        compiler_params=pltpu.CompilerParams(
            collective_id=0, has_side_effects=True, vmem_limit_bytes=57 * 2**20
        ),
    )(grad_out, layer_input, router_weight, expert_ids.T, gate_probs.T, eo)
    grows, gin, grout = pl.pallas_call(
        writer,
        out_shape=(
            jax.ShapeDtypeStruct((ROWS, 64, D), BF),
            jax.ShapeDtypeStruct((TOK, D), BF),
            jax.ShapeDtypeStruct((D, EXP), F32),
        ),
        in_specs=[hbm] * 3,
        out_specs=(hbm, hbm, hbm),
        scratch_shapes=[
            vm((ROWS, 64, D), BF), vm((TOK, D), BF), vm((8, 256, EXP), BF), vm((D, EXP), F32),
            sem((8,)), sem((3,)),
        ],
        compiler_params=pltpu.CompilerParams(vmem_limit_bytes=57 * 2**20),
    )(*results)
    grows = grows.reshape(2, CAP, 64, D).transpose(0, 2, 1, 3)
    return grows[None], gin, grout


def solution(mesh):
    return jax.shard_map(
        body,
        mesh=mesh,
        in_specs=(
            P(("dp", "expert"), None),
            P(("dp", "expert"), None),
            P(),
            P(("dp", "expert"), None),
            P(("dp", "expert"), None),
            P("dp", "expert", None, None, None),
        ),
        out_specs=(P("dp", "expert", None, None, None), P(("dp", "expert"), None), P()),
        check_vma=False,
    )
```

```python
import jax
import jax.numpy as jnp
from jax import lax
from jax.experimental import pallas as pl
from jax.experimental.pallas import tpu as pltpu
from jax.sharding import PartitionSpec as P

MESH = pl.DeviceIdType.MESH
BF, F32 = jnp.bfloat16, jnp.float32
NX, NZ, NY = 4, 8, 4
D, TOK, TOP, EXP, CAP = 2048, 128, 8, 128, 9
ROWS = 2 * CAP
UNITS, UW, WID = 8, 128, 256
RING = 7
HOPS = ((4, 3), (3, 4))
STEP, HOP = 4.8, 3.3
ORDER = (0, 1, 2, 3, 4, 5, 7, 6)
ACROSS = tuple((dz, dc) for dz in (4, 3, 5, 2, 6, 1, 7) for dc in range(2)) + ((0, 1),)
SPREAD = {(5, 4): 2, (6, 3): 13}
REL = ((2, 0), (2, 1), (1, 0), (3, 0), (1, 1), (3, 1), (0, 1), (0, 0))


def iota(shape, axis):
    return lax.broadcasted_iota(jnp.int32, shape, axis)


def dot(a, b, dims=((1,), (0,))):
    return lax.dot_general(a, b, (dims, ((), ())), preferred_element_type=F32)


def earlier():
    return (iota((TOK, TOK), 0) < iota((TOK, TOK), 1)).astype(BF)


def kernel(
    go, li, rw_in, ids_in, gates_in, eo, grows, gin_out, agb_out,
    x_buf, f_buf, o_buf, w_buf, r_buf, gin, agb, e_buf, rw, ids_own, gates_own, meta, mb, slots, gates, m_buf, mb2, g2_buf, w2_buf, f2_buf, o2_buf, h_in, turn, mb3, few, fews,
    own_slot, own_gate, acc, s_out, t_in, count, lib, lit, glt, glb, part, rb, fin, ag, half,
    loc, xch_s, xch_r, ring_s, ring_r, meta_s, meta_r, li_s, li_r, x_s, x_r, h_s, h_r, h2_s, h2_r, h3_s, h3_r, h4_s, h4_r,
    sc_s, sc_r, gl_s, gl_r, rs_s, rs_r, a1_s, a1_r, a2_s, a2_r, a3_s, a3_r,
):
    y = lax.axis_index("dp")
    idx = lax.axis_index("expert")
    x, z, c = idx // 16, (idx // 2) % NZ, idx % 2

    def at(dx=0, dy=0, dz=0, dc=0):
        xx, zz, cc = lax.rem(x + dx, NX), lax.rem(z + dz, NZ), lax.rem(c + dc, 2)
        return (lax.rem(y + dy, NY), xx * 16 + zz * 2 + cc)

    def bulk(ref, n, s):
        pltpu.make_async_copy(ref.at[pl.ds(0, n)], ref.at[pl.ds(0, n)], s).wait()

    def taken(ref, s):
        pltpu.make_async_copy(ref, ref, s).wait()

    def send(src, dst, ss, rs, to):
        return pltpu.make_async_remote_copy(
            src_ref=src, dst_ref=dst, send_sem=ss, recv_sem=rs, device_id=to, device_id_type=MESH
        )

    load_ids = pltpu.make_async_copy(ids_in, ids_own, loc.at[6])
    load_ids.start()
    load_gates = pltpu.make_async_copy(gates_in, gates_own, loc.at[2])
    load_gates.start()
    load_e = pltpu.make_async_copy(eo, e_buf, loc.at[0])
    load_e.start()
    own_half = []
    for u in range(UNITS):
        cols = pl.ds(pl.multiple_of(c * 1024 + u * UW, UW), UW)
        cp = pltpu.make_async_copy(go.at[:, cols], x_buf.at[u, 2 * z + c], loc.at[7 + u])
        cp.start()
        own_half.append(cp)
    own_li = pltpu.make_async_copy(
        li.at[:, pl.ds(pl.multiple_of((2 * y + c) * WID, WID), WID)], lib.at[2 * y + c], loc.at[5]
    )
    own_li.start()
    load_rw = pltpu.make_async_copy(rw_in, rw, loc.at[3])
    load_rw.start()

    barrier = pltpu.get_barrier_semaphore()
    zc = [(dz, dc) for dz in range(NZ) for dc in range(2) if dz or dc]
    yc = [(dy, dc) for dy in range(NY) for dc in range(2) if dy or dc]
    greet = [dict(dz=a, dc=b) for a, b in zc]
    greet += [dict(dx=a, dc=b) for a, b in REL if a]
    greet += [dict(dy=a, dc=b) for a, b in yc if a]
    for g in greet:
        pl.semaphore_signal(barrier, inc=1, device_id=at(**g), device_id_type=MESH)
    load_ids.wait()
    load_gates.wait()
    meta[0:TOP, :] = ids_own[...].astype(F32).astype(BF)
    meta[TOP:, :] = gates_own[...].astype(BF)
    mb[pl.ds(2 * z + c, 1)] = meta[...].reshape(1, 2 * TOP, TOK)
    pl.semaphore_wait(barrier, len(greet))


    swap = []
    for u in range(UNITS):
        cols = pl.ds(pl.multiple_of((1 - c) * 1024 + u * UW, UW), UW)
        swap.append(
            send(go.at[:, cols], x_buf.at[u, 2 * z + c], xch_s, xch_r.at[u], at(dc=1))
        )
    swap[0].start()
    swap[RING].start()
    swap[1].start()

    def came(d, h):
        return lax.rem(z + (NZ - h if d == 0 else h), NZ)

    def ring(u, d, h):
        blk = x_buf.at[u, pl.ds(2 * came(d, h - 1), 2)]
        return send(
            blk, blk, ring_s, ring_r.at[u, d, h - 1],
            at(dz=1 if d == 0 else NZ - 1),
        )

    def landed(u, d, h):
        blk = x_buf.at[u, pl.ds(2 * came(d, h), 2)]
        send(
            blk, blk, ring_s, ring_r.at[u, d, h - 1],
            at(dz=1 if d == 0 else NZ - 1),
        ).wait_recv()

    def ring0(d, h, i):
        blk = x_buf.at[0, pl.ds(2 * came(d, h - 1) + (c if i == 0 else 1 - c), 1)]
        return send(
            blk, blk, ring_s, ring_r.at[RING * i, d, h - 1], at(dz=1 if d == 0 else NZ - 1)
        )

    def landed0(d, h, i):
        blk = x_buf.at[0, pl.ds(2 * came(d, h) + (c if i == 0 else 1 - c), 1)]
        send(
            blk, blk, ring_s, ring_r.at[RING * i, d, h - 1], at(dz=1 if d == 0 else NZ - 1)
        ).wait_recv()

    def hop0(h):
        for i in range(2):
            if h == 0 and i == 0:
                own_half[0].wait()
            if h == 0 and i == 1:
                swap[0].wait_recv()
            for d in range(2):
                if 0 < h < 4 or h == 4 and d == i:
                    landed0(d, h, i)
                if h < 3 or h == 3 and d == i:
                    ring0(d, h + 1, i).start()

    def hop(u, h):
        if u == 0:
            hop0(h)
            return
        if h == 0:
            own_half[u].wait()
            swap[u].wait_recv()
        for d in range(2):
            if 0 < h <= HOPS[u % 2][d]:
                landed(u, d, h)
            if h < HOPS[u % 2][d]:
                cp = ring(u, d, h + 1)
                cp.start()

    steps = sorted((u * STEP + h * HOP, u, h) for u in range(RING) for h in range(5))
    steps = [(u, h) for _, u, h in steps]
    hop(*steps[0])

    for i, (dz, dc) in enumerate(zc):
        cp = send(meta, mb.at[2 * z + c], meta_s, meta_r, at(dz=dz, dc=dc))
        cp.start()
    for u in range(2, RING):
        swap[u].start()
    for dy, dc in yc:
        send(meta, mb3.at[2 * y + c], h4_s, h4_r, at(dy=dy, dc=dc)).start()
    mb3[pl.ds(2 * y + c, 1)] = meta[...].reshape(1, 2 * TOP, TOK)

    own_half[RING].wait()
    swap[RING].wait_recv()
    for i in range(1, NX):
        cp = send(x_buf.at[RING, pl.ds(2 * z, 2)], g2_buf.at[pl.ds(2 * x, 2)], h_s, h_r, at(dx=i))
        cp.start()
    xc = [(dx, dc) for dx, dc in REL if dx]
    for i, (dx, dc) in enumerate(xc):
        cp = send(meta, mb2.at[2 * x + c], h2_s, h2_r, at(dx=dx, dc=dc))
        cp.start()
    g2_buf[pl.ds(2 * x, 2)] = x_buf[RING, pl.ds(2 * z, 2)]

    lane_row = iota((TOK, TOK), 0)
    expert = 2 * lax.rem(lane_row, 64) + lane_row // 64
    named = jnp.zeros((EXP, TOK), F32)
    gate = jnp.zeros((EXP, TOK), F32)
    for k in range(TOP):
        hit = ids_own[k : k + 1, :] == expert
        named = jnp.where(hit, 1.0, named)
        gate = jnp.where(hit, gates_own[k : k + 1, :], gate)
    before = dot(named.astype(BF), earlier())
    own_slot[...] = jnp.where(named > 0, before, 99.0)
    own_gate[...] = gate

    li_cp = []
    for i, (dy, dc) in enumerate(yc):
        g = 2 * lax.rem(y + dy, NY) + lax.rem(c + dc, 2)
        cp = send(
            li.at[:, pl.ds(pl.multiple_of(g * WID, WID), WID)], lib.at[2 * y + c],
            li_s, li_r, at(dy=dy, dc=dc),
        )
        li_cp.append(cp)

    def tables():
        bulk(mb, 15, meta_r)
        row = iota((16, TOK), 0)
        here = (row // 4) * 32 + z * 4 + lax.rem(row, 4)
        for j in range(16):
            ids = mb[j, 0:TOP, :].astype(F32).astype(jnp.int32)
            gts = mb[j, TOP:, :].astype(F32)
            nm = jnp.zeros((16, TOK), F32)
            gt = jnp.zeros((16, TOK), F32)
            for k in range(TOP):
                hit = ids[k : k + 1, :] == here
                nm = jnp.where(hit, 1.0, nm)
                gt = jnp.where(hit, gts[k : k + 1, :], gt)
            m_buf[j * 16 : (j + 1) * 16, :] = nm
            gates[j * 16 : (j + 1) * 16, :] = gt
        bef = dot(m_buf[...].astype(BF), earlier())
        slots[...] = jnp.where(m_buf[...] > 0, bef, 99.0)

        def one(j, carry):
            base = pl.multiple_of(j * 16, 16)
            sl = slots[pl.ds(base, 16), :]
            gt = gates[pl.ds(base, 16), :]
            for s in range(CAP):
                w_buf[j, s * 16 : (s + 1) * 16, :] = jnp.where(sl == float(s), gt, 0.0).astype(BF)
            return carry

        lax.fori_loop(0, 16, one, 0)

    def block(u, zb):
        for i in range(2):
            j = 2 * zb + i
            got = dot(w_buf[j], x_buf[u, j])
            for s in range(CAP):
                f_buf[u % 4, pl.ds(s * 16 + j, 16, stride=CAP * 16), :] = got[s * 16 : (s + 1) * 16, :]

    def place(u, xs, cs):
        cols = pl.ds(pl.multiple_of(cs * 1024 + u * UW, UW), UW)
        return r_buf.at[:, pl.ds(pl.multiple_of(xs * 16, 16), 16), cols]

    out_cp = []

    def rows(u, a):
        dx, dc = REL[a]
        xd, cd = lax.rem(x + dx, NX), lax.rem(c + dc, 2)
        base = pl.multiple_of((xd * 2 + cd) * (ROWS * 16), 32)
        o_buf[u, a] = f_buf[u % 4, pl.ds(base, ROWS * 16), :].astype(BF).reshape(ROWS, 16, UW)
        if a < 7:
            cp = send(o_buf.at[u, a], place(u, x, c), x_s, x_r.at[u], at(dx=dx, dc=dc))
        else:
            cp = pltpu.make_async_copy(o_buf.at[u, a], place(u, x, c), loc.at[15 + u])
            out_cp.append(cp)
        cp.start()

    def across():
        bulk(g2_buf, 6, h_r)
        bulk(mb2, 6, h2_r)
        mb2[pl.ds(2 * x, 2)] = mb[pl.ds(2 * z, 2)]
        here = x * 32 + iota((32, TOK), 0)
        for j in range(8):
            ids = mb2[j, 0:TOP, :].astype(F32).astype(jnp.int32)
            gts = mb2[j, TOP:, :].astype(F32)
            nm = jnp.zeros((32, TOK), F32)
            gt = jnp.zeros((32, TOK), F32)
            for k in range(TOP):
                hit = ids[k : k + 1, :] == here
                nm = jnp.where(hit, 1.0, nm)
                gt = jnp.where(hit, gts[k : k + 1, :], gt)
            m_buf[j * 32 : (j + 1) * 32, :] = nm
            gates[j * 32 : (j + 1) * 32, :] = gt
        bef = dot(m_buf[...].astype(BF), earlier())
        slots[...] = jnp.where(m_buf[...] > 0, bef, 99.0)
        for j in range(8):
            sl = slots[j * 32 : (j + 1) * 32, :]
            gt = gates[j * 32 : (j + 1) * 32, :]
            for s in range(CAP):
                w2_buf[j, s * 32 : (s + 1) * 32, :] = jnp.where(sl == float(s), gt, 0.0).astype(BF)
        for j in range(8):
            got = dot(w2_buf[j], g2_buf[j])
            for s in range(CAP):
                f2_buf[pl.ds(s * 8 + j, 32, stride=CAP * 8), :] = got[s * 32 : (s + 1) * 32, :]
        o2_buf[...] = f2_buf[...].astype(BF).reshape(16, ROWS * 8, UW)
        h_in[pl.ds(2 * z + c, 1)] = o2_buf[pl.ds(2 * z + c, 1)]
        to, fr = iota((128, 128), 0), iota((128, 128), 1)
        q = lax.rem(to, 64)
        want = (lax.rem(q, 16) // 2) * 16 + (to // 64) * 8 + (q // 16) * 2 + lax.rem(q, 2)
        turn[...] = (fr == want).astype(BF)

    h3_cp = []

    def across_send(n):
        for _ in range(n):
            i = len(h3_cp)
            if i == len(zc):
                return
            dz, dc = ACROSS[i]
            to = 2 * lax.rem(z + dz, NZ) + lax.rem(c + dc, 2)
            cp = send(o2_buf.at[to], h_in.at[2 * z + c], h3_s, h3_r, at(dz=dz, dc=dc))
            cp.start()
            h3_cp.append(cp)

    def across_done():
        bulk(h_in, 15, h3_r)
        for t in range(CAP):
            tile = pl.ds(t * 16, 16)
            both = [
                jnp.concatenate([h_in[2 * k + h, tile, :] for k in range(NZ)], axis=0) for h in range(2)
            ]
            got = dot(turn[...], jnp.concatenate(both, axis=1)).astype(BF)
            for h in range(2):
                col = h * 1024 + RING * UW
                r_buf[2 * t : 2 * t + 2, :, col : col + UW] = got[:, h * UW : (h + 1) * UW].reshape(2, 64, UW)

    def work(u, h):
        if h == 0:
            block(u, z)
        for d in range(2):
            if 0 < h <= HOPS[u % 2][d]:
                block(u, came(d, h))
        if h == 4:
            for a in range(8):
                rows(u, a)
            if u == 1:
                across()

    late = [steps[0]]
    for n, (u, h) in enumerate(steps[1:]):
        hop(u, h)
        late.append((u, h))
        across_send(SPREAD.get((u, h), 0))
        if n == 2:
            for cp in li_cp:
                cp.start()
            tables()
        if n >= 2:
            for q in late:
                work(*q)
            late = []

    own_li.wait()
    bulk(lib, 7, li_r)
    eye = (iota((TOK, TOK), 0) == iota((TOK, TOK), 1)).astype(BF)
    for g in range(8):
        lit[:, g * TOK : (g + 1) * TOK] = dot(lib[g], eye, ((0,), (0,))).astype(BF)

    load_e.wait()
    for u in ORDER:
        if u == RING:
            across_done()
        else:
            taken(o_buf.at[u, pl.ds(0, 7)], x_r.at[u])
            out_cp[u].wait()
        for h in range(2):
            cols = pl.ds(h * 1024 + u * UW, UW)
            cp = pltpu.make_async_copy(r_buf.at[:, :, cols], grows.at[:, :, cols], loc.at[0])
            cp.start()

        def score(r, carry, u=u):
            tot = jnp.zeros((64, 128), F32)
            for h in range(2):
                col = h * 1024 + u * UW
                a = r_buf[r, :, col : col + 128].astype(F32)
                b = e_buf[r, :, col : col + 128].astype(F32)
                tot = tot + a * b
            acc[r] = tot if u == 0 else acc[r] + tot
            return carry

        lax.fori_loop(0, ROWS, score, 0)

    total = jnp.zeros((64, 128), F32)
    for r in range(ROWS):
        total = jnp.where(iota((64, 128), 1) == r, jnp.sum(acc[r], axis=1, keepdims=True), total)
    s_out[...] = total

    def sc(i):
        to = lax.rem(idx + i, 64)
        return send(s_out.at[pl.ds(to, 1)], t_in.at[pl.ds(idx, 1)], sc_s, sc_r, (y, to))

    def sc_start(i, carry):
        sc(i).start()
        return carry

    lax.fori_loop(1, 64, sc_start, 0)
    t_in[pl.ds(idx, 1)] = s_out[pl.ds(idx, 1)]
    taken(x_buf.at[:, 0], xch_s)
    taken(x_buf.at[pl.ds(0, RING), pl.ds(0, 14)], ring_s)
    taken(o_buf.at[pl.ds(0, RING), pl.ds(0, 7)], x_s)
    bulk(mb, 15, meta_s)
    bulk(lib, 7, li_s)
    bulk(g2_buf, 6, h_s)
    bulk(mb2, 6, h2_s)
    bulk(h_in, 15, h3_s)
    bulk(mb3, 7, h4_s)
    bulk(mb3, 7, h4_r)
    taken(count, sc_r)

    back = t_in[...]
    scaled = []
    for l in range(2):
        sl = own_slot[l * 64 : (l + 1) * 64, :]
        v = jnp.zeros((64, TOK), F32)
        for s in range(CAP):
            v = jnp.where(sl == float(s), back[:, l * CAP + s : l * CAP + s + 1], v)
        scaled.append(v)
    scaled = jnp.concatenate(scaled, axis=0)
    total = jnp.sum(scaled, axis=0, keepdims=True)
    for k in range(TOP):
        mine = jnp.sum(jnp.where(ids_own[k : k + 1, :] == expert, scaled, 0.0), axis=0, keepdims=True)
        few[k : k + 1, :] = mine - gates_own[k : k + 1, :] * total

    for dy, dc in yc:
        send(few, fews.at[2 * y + c], gl_s, gl_r, at(dy=dy, dc=dc)).start()
    fews[pl.ds(2 * y + c, 1)] = few[...].reshape(1, TOP, TOK)

    def spread(ids, vals):
        got = jnp.zeros((EXP, TOK), F32)
        for k in range(TOP):
            got = jnp.where(ids[k : k + 1, :] == lane_row, vals[k : k + 1, :], got)
        return got.astype(BF)

    glt[...] = spread(ids_own[...], few[...])
    load_rw.wait()
    gin[...] = dot(glt[...], rw[...], ((0,), (1,))).astype(BF)
    pltpu.make_async_copy(gin, gin_out, loc.at[1]).start()
    bulk(fews, 7, gl_r)
    for j in range(8):
        glb[:, j * TOK : (j + 1) * TOK] = spread(mb3[j, 0:TOP, :].astype(F32).astype(jnp.int32), fews[j])
    part[...] = dot(lit[...], glb[...], ((1,), (1,))).astype(BF)

    chip = x * NZ + z
    seat = x * 4 + z // 2
    owner = lax.rem(z, 2) == 0

    def seat_at(q):
        return (y, (q // 4) * 16 + lax.rem(q, 4) * 4 + c)

    def rs_start(i, carry):
        q = lax.rem(seat + i, 16)
        send(
            part.at[pl.ds(pl.multiple_of(q * 16, 16), 16)], rb.at[chip], rs_s, rs_r, seat_at(q)
        ).start()
        return carry

    def a1_start(i, carry):
        q = lax.rem(chip + i, 32)
        send(fin, ag.at[seat], a1_s, a1_r, (y, q * 2 + c)).start()
        return carry

    lax.fori_loop(1, 16, rs_start, 0)

    @pl.when(owner)
    def _():
        rb[pl.ds(chip, 1)] = part[pl.ds(pl.multiple_of(seat * 16, 16), 16), :].reshape(1, 16, EXP)
        taken(count, sc_s)
        bulk(fews, 7, gl_s)
        bulk(rb, 31, rs_r)
        fin[...] = jnp.sum(rb[...].astype(F32), axis=0).astype(BF)
        lax.fori_loop(1, 32, a1_start, 0)
        ag[pl.ds(seat, 1)] = fin[...].reshape(1, 16, EXP)
        bulk(rb, 15, rs_s)
        bulk(ag, 15, a1_r)

    @pl.when(jnp.logical_not(owner))
    def _():
        rs_start(0, 0)
        taken(count, sc_s)
        bulk(fews, 7, gl_s)
        bulk(rb, 16, rs_s)
        bulk(ag, 16, a1_r)

    half[...] = ag[...].reshape(256, EXP)

    for i in range(1, NY):
        cp = send(half, agb.at[2 * y + c], a2_s, a2_r.at[i], at(dy=i))
        cp.start()

    def swap_part(g, src):
        send(src, agb.at[g], a3_s, a3_r, at(dc=1)).start()

    swap_part(2 * y + c, half)
    agb[pl.ds(2 * y + c, 1)] = half[...].reshape(1, 256, EXP)

    @pl.when(owner)
    def _():
        bulk(rb, 31, a1_s)

    taken(r_buf, loc.at[0])
    taken(gin, loc.at[1])
    for i in range(1, NY):
        ys = lax.rem(y + NY - i, NY)
        send(half, agb.at[2 * ys + c], a2_s, a2_r.at[i], at(dy=i)).wait_recv()
        swap_part(2 * ys + c, agb.at[2 * ys + c])
    bulk(agb, NY, a3_r)
    store = pltpu.make_async_copy(agb, agb_out, loc.at[0])
    store.start()
    bulk(agb, NY - 1, a2_s)
    bulk(agb, NY, a3_s)
    store.wait()


def writer(rows_in, gin_in, agb_in, grows, gin_out, grout, rows, gin, parts, wide, loc, sto):
    pieces = [pl.ds(3 * i, 3) for i in range(6)]
    loads = [pltpu.make_async_copy(agb_in, parts, loc.at[6]), pltpu.make_async_copy(gin_in, gin, loc.at[7])]
    loads += [pltpu.make_async_copy(rows_in.at[p], rows.at[p], loc.at[i]) for i, p in enumerate(pieces)]
    for cp in loads:
        cp.start()
    loads[0].wait()
    wide[...] = parts[...].reshape(D, EXP).astype(F32)
    pltpu.make_async_copy(wide, grout, sto.at[0]).start()
    loads[1].wait()
    pltpu.make_async_copy(gin, gin_out, sto.at[1]).start()
    for i, p in enumerate(pieces):
        loads[2 + i].wait()
        pltpu.make_async_copy(rows.at[p], grows.at[p], sto.at[2]).start()
    pltpu.make_async_copy(wide, grout, sto.at[0]).wait()
    pltpu.make_async_copy(gin, gin_out, sto.at[1]).wait()
    pltpu.make_async_copy(rows, grows, sto.at[2]).wait()


def body(grad_out, layer_input, router_weight, gate_probs, expert_ids, expert_out):
    eo = expert_out[0].transpose(0, 2, 1, 3).reshape(ROWS, 64, D)
    vm, sem = pltpu.VMEM, pltpu.SemaphoreType.DMA
    hbm = pl.BlockSpec(memory_space=pltpu.HBM)
    results = pl.pallas_call(
        kernel,
        out_shape=(
            jax.ShapeDtypeStruct((ROWS, 64, D), BF),
            jax.ShapeDtypeStruct((TOK, D), BF),
            jax.ShapeDtypeStruct((8, 256, EXP), BF),
        ),
        in_specs=[hbm] * 6,
        out_specs=(hbm, hbm, hbm),
        scratch_shapes=[
            vm((UNITS, 16, TOK, UW), BF),
            vm((4, 8 * ROWS * 16, UW), F32),
            vm((UNITS, 8, ROWS, 16, UW), BF),
            vm((16, CAP * 16, TOK), BF),
            vm((ROWS, 64, D), BF),
            vm((TOK, D), BF),
            vm((8, 256, EXP), BF),
            vm((ROWS, 64, D), BF),
            vm((D, EXP), BF),
            vm((TOP, TOK), jnp.int32),
            vm((TOP, TOK), F32),
            vm((2 * TOP, TOK), BF),
            vm((16, 2 * TOP, TOK), BF),
            vm((256, TOK), F32),
            vm((256, TOK), F32),
            vm((256, TOK), F32),
            vm((8, 2 * TOP, TOK), BF),
            vm((8, TOK, UW), BF),
            vm((8, CAP * 32, TOK), BF),
            vm((16 * ROWS * 8, UW), F32),
            vm((16, ROWS * 8, UW), BF),
            vm((16, ROWS * 8, UW), BF),
            vm((128, 128), BF),
            vm((8, 2 * TOP, TOK), BF),
            vm((TOP, TOK), F32),
            vm((8, TOP, TOK), F32),
            vm((EXP, TOK), F32),
            vm((EXP, TOK), F32),
            vm((ROWS, 64, 128), F32),
            vm((64, 128), F32),
            vm((64, 128), F32),
            vm((63, 1, 128), F32),
            vm((8, TOK, WID), BF),
            vm((WID, 8 * TOK), BF),
            vm((EXP, TOK), BF),
            vm((EXP, 8 * TOK), BF),
            vm((WID, EXP), BF),
            vm((32, 16, EXP), BF),
            vm((16, EXP), BF),
            vm((16, 16, EXP), BF),
            vm((256, EXP), BF),
            sem((22,)),
            sem, sem((UNITS,)),
            sem, sem((RING + 1, 2, 4)),
            sem, sem,
            sem, sem,
            sem, sem((RING,)),
            sem, sem, sem, sem, sem, sem, sem, sem,
            sem, sem,
            sem, sem,
            sem, sem,
            sem, sem,
            sem, sem((NY,)),
            sem, sem,
        ],
        compiler_params=pltpu.CompilerParams(
            collective_id=0, has_side_effects=True, vmem_limit_bytes=57 * 2**20
        ),
    )(grad_out, layer_input, router_weight, expert_ids.T, gate_probs.T, eo)
    grows, gin, grout = pl.pallas_call(
        writer,
        out_shape=(
            jax.ShapeDtypeStruct((ROWS, 64, D), BF),
            jax.ShapeDtypeStruct((TOK, D), BF),
            jax.ShapeDtypeStruct((D, EXP), F32),
        ),
        in_specs=[hbm] * 3,
        out_specs=(hbm, hbm, hbm),
        scratch_shapes=[
            vm((ROWS, 64, D), BF), vm((TOK, D), BF), vm((8, 256, EXP), BF), vm((D, EXP), F32),
            sem((8,)), sem((3,)),
        ],
        compiler_params=pltpu.CompilerParams(vmem_limit_bytes=57 * 2**20),
    )(*results)
    grows = grows.reshape(2, CAP, 64, D).transpose(0, 2, 1, 3)
    return grows[None], gin, grout


def solution(mesh):
    return jax.shard_map(
        body,
        mesh=mesh,
        in_specs=(
            P(("dp", "expert"), None),
            P(("dp", "expert"), None),
            P(),
            P(("dp", "expert"), None),
            P(("dp", "expert"), None),
            P("dp", "expert", None, None, None),
        ),
        out_specs=(P("dp", "expert", None, None, None), P(("dp", "expert"), None), P()),
        check_vma=False,
    )
```

```python
import jax
import jax.numpy as jnp
from jax import lax
from jax.experimental import pallas as pl
from jax.experimental.pallas import tpu as pltpu
from jax.sharding import PartitionSpec as P

MESH = pl.DeviceIdType.MESH
BF, F32 = jnp.bfloat16, jnp.float32
NX, NZ, NY = 4, 8, 4
D, TOK, TOP, EXP, CAP = 2048, 128, 8, 128, 9
ROWS = 2 * CAP
UNITS, UW, WID = 8, 128, 256
RING = 7
HOPS = ((4, 3), (3, 4))
STEP, HOP = 4.8, 3.3
ORDER = (0, 1, 2, 3, 4, 5, 7, 6)
ACROSS = tuple((dz, dc) for dz in (4, 3, 5, 2, 6, 1, 7) for dc in range(2)) + ((0, 1),)
SPREAD = {(5, 4): 2, (6, 3): 13}
REL = ((2, 0), (2, 1), (1, 0), (3, 0), (1, 1), (3, 1), (0, 1), (0, 0))


def iota(shape, axis):
    return lax.broadcasted_iota(jnp.int32, shape, axis)


def dot(a, b, dims=((1,), (0,))):
    return lax.dot_general(a, b, (dims, ((), ())), preferred_element_type=F32)


def earlier():
    return (iota((TOK, TOK), 0) < iota((TOK, TOK), 1)).astype(BF)


def kernel(
    go, li, rw_in, ids_in, gates_in, eo, grows, gin_out, agb_out,
    x_buf, f_buf, o_buf, w_buf, r_buf, gin, agb, e_buf, rw, ids_own, gates_own, meta, mb, slots, gates, m_buf, mb2, g2_buf, w2_buf, f2_buf, o2_buf, h_in, turn, mb3, few, fews,
    own_slot, own_gate, acc, s_out, t_in, count, lib, lit, glt, glb, part, rb, fin, ag, half,
    loc, xch_s, xch_r, ring_s, ring_r, meta_s, meta_r, li_s, li_r, x_s, x_r, h_s, h_r, h2_s, h2_r, h3_s, h3_r, h4_s, h4_r,
    sc_s, sc_r, gl_s, gl_r, rs_s, rs_r, a1_s, a1_r, a2_s, a2_r, a3_s, a3_r,
):
    y = lax.axis_index("dp")
    idx = lax.axis_index("expert")
    x, z, c = idx // 16, (idx // 2) % NZ, idx % 2

    def at(dx=0, dy=0, dz=0, dc=0):
        xx, zz, cc = lax.rem(x + dx, NX), lax.rem(z + dz, NZ), lax.rem(c + dc, 2)
        return (lax.rem(y + dy, NY), xx * 16 + zz * 2 + cc)

    def bulk(ref, n, s):
        pltpu.make_async_copy(ref.at[pl.ds(0, n)], ref.at[pl.ds(0, n)], s).wait()

    def taken(ref, s):
        pltpu.make_async_copy(ref, ref, s).wait()

    def send(src, dst, ss, rs, to):
        return pltpu.make_async_remote_copy(
            src_ref=src, dst_ref=dst, send_sem=ss, recv_sem=rs, device_id=to, device_id_type=MESH
        )

    load_ids = pltpu.make_async_copy(ids_in, ids_own, loc.at[6])
    load_ids.start()
    load_gates = pltpu.make_async_copy(gates_in, gates_own, loc.at[2])
    load_gates.start()
    load_e = pltpu.make_async_copy(eo, e_buf, loc.at[0])
    load_e.start()
    own_half = []
    for u in range(UNITS):
        cols = pl.ds(pl.multiple_of(c * 1024 + u * UW, UW), UW)
        cp = pltpu.make_async_copy(go.at[:, cols], x_buf.at[u, 2 * z + c], loc.at[7 + u])
        cp.start()
        own_half.append(cp)
    own_li = pltpu.make_async_copy(
        li.at[:, pl.ds(pl.multiple_of((2 * y + c) * WID, WID), WID)], lib.at[2 * y + c], loc.at[5]
    )
    own_li.start()
    load_rw = pltpu.make_async_copy(rw_in, rw, loc.at[3])
    load_rw.start()

    barrier = pltpu.get_barrier_semaphore()
    zc = [(dz, dc) for dz in range(NZ) for dc in range(2) if dz or dc]
    yc = [(dy, dc) for dy in range(NY) for dc in range(2) if dy or dc]
    greet = [dict(dz=a, dc=b) for a, b in zc]
    greet += [dict(dx=a, dc=b) for a, b in REL if a]
    greet += [dict(dy=a, dc=b) for a, b in yc if a]
    for g in greet:
        pl.semaphore_signal(barrier, inc=1, device_id=at(**g), device_id_type=MESH)
    load_ids.wait()
    load_gates.wait()
    meta[0:TOP, :] = ids_own[...].astype(F32).astype(BF)
    meta[TOP:, :] = gates_own[...].astype(BF)
    mb[pl.ds(2 * z + c, 1)] = meta[...].reshape(1, 2 * TOP, TOK)
    pl.semaphore_wait(barrier, len(greet))


    swap = []
    for u in range(UNITS):
        cols = pl.ds(pl.multiple_of((1 - c) * 1024 + u * UW, UW), UW)
        swap.append(
            send(go.at[:, cols], x_buf.at[u, 2 * z + c], xch_s, xch_r.at[u], at(dc=1))
        )
    swap[0].start()
    swap[RING].start()
    swap[1].start()

    def came(d, h):
        return lax.rem(z + (NZ - h if d == 0 else h), NZ)

    def ring(u, d, h):
        blk = x_buf.at[u, pl.ds(2 * came(d, h - 1), 2)]
        return send(
            blk, blk, ring_s, ring_r.at[u, d, h - 1],
            at(dz=1 if d == 0 else NZ - 1),
        )

    def landed(u, d, h):
        blk = x_buf.at[u, pl.ds(2 * came(d, h), 2)]
        send(
            blk, blk, ring_s, ring_r.at[u, d, h - 1],
            at(dz=1 if d == 0 else NZ - 1),
        ).wait_recv()

    def ring0(d, h, i):
        blk = x_buf.at[0, pl.ds(2 * came(d, h - 1) + (c if i == 0 else 1 - c), 1)]
        return send(
            blk, blk, ring_s, ring_r.at[RING * i, d, h - 1], at(dz=1 if d == 0 else NZ - 1)
        )

    def landed0(d, h, i):
        blk = x_buf.at[0, pl.ds(2 * came(d, h) + (c if i == 0 else 1 - c), 1)]
        send(
            blk, blk, ring_s, ring_r.at[RING * i, d, h - 1], at(dz=1 if d == 0 else NZ - 1)
        ).wait_recv()

    def hop0(h):
        for i in range(2):
            if h == 0 and i == 0:
                own_half[0].wait()
            if h == 0 and i == 1:
                swap[0].wait_recv()
            for d in range(2):
                if 0 < h < 4 or h == 4 and d == i:
                    landed0(d, h, i)
                if h < 3 or h == 3 and d == i:
                    ring0(d, h + 1, i).start()

    def hop(u, h):
        if u == 0:
            hop0(h)
            return
        if h == 0:
            own_half[u].wait()
            swap[u].wait_recv()
        for d in range(2):
            if 0 < h <= HOPS[u % 2][d]:
                landed(u, d, h)
            if h < HOPS[u % 2][d]:
                cp = ring(u, d, h + 1)
                cp.start()

    steps = sorted((u * STEP + h * HOP, u, h) for u in range(RING) for h in range(5))
    steps = [(u, h) for _, u, h in steps]
    hop(*steps[0])

    for i, (dz, dc) in enumerate(zc):
        cp = send(meta, mb.at[2 * z + c], meta_s, meta_r, at(dz=dz, dc=dc))
        cp.start()
    for u in range(2, RING):
        swap[u].start()
    for dy, dc in yc:
        send(meta, mb3.at[2 * y + c], h4_s, h4_r, at(dy=dy, dc=dc)).start()
    mb3[pl.ds(2 * y + c, 1)] = meta[...].reshape(1, 2 * TOP, TOK)

    own_half[RING].wait()
    swap[RING].wait_recv()
    for i in range(1, NX):
        cp = send(x_buf.at[RING, pl.ds(2 * z, 2)], g2_buf.at[pl.ds(2 * x, 2)], h_s, h_r, at(dx=i))
        cp.start()
    xc = [(dx, dc) for dx, dc in REL if dx]
    for i, (dx, dc) in enumerate(xc):
        cp = send(meta, mb2.at[2 * x + c], h2_s, h2_r, at(dx=dx, dc=dc))
        cp.start()
    g2_buf[pl.ds(2 * x, 2)] = x_buf[RING, pl.ds(2 * z, 2)]

    lane_row = iota((TOK, TOK), 0)
    expert = 2 * lax.rem(lane_row, 64) + lane_row // 64
    named = jnp.zeros((EXP, TOK), F32)
    gate = jnp.zeros((EXP, TOK), F32)
    for k in range(TOP):
        hit = ids_own[k : k + 1, :] == expert
        named = jnp.where(hit, 1.0, named)
        gate = jnp.where(hit, gates_own[k : k + 1, :], gate)
    before = dot(named.astype(BF), earlier())
    own_slot[...] = jnp.where(named > 0, before, 99.0)
    own_gate[...] = gate

    li_cp = []
    for i, (dy, dc) in enumerate(yc):
        g = 2 * lax.rem(y + dy, NY) + lax.rem(c + dc, 2)
        cp = send(
            li.at[:, pl.ds(pl.multiple_of(g * WID, WID), WID)], lib.at[2 * y + c],
            li_s, li_r, at(dy=dy, dc=dc),
        )
        li_cp.append(cp)

    def tables():
        bulk(mb, 15, meta_r)
        row = iota((16, TOK), 0)
        here = (row // 4) * 32 + z * 4 + lax.rem(row, 4)
        for j in range(16):
            ids = mb[j, 0:TOP, :].astype(F32).astype(jnp.int32)
            gts = mb[j, TOP:, :].astype(F32)
            nm = jnp.zeros((16, TOK), F32)
            gt = jnp.zeros((16, TOK), F32)
            for k in range(TOP):
                hit = ids[k : k + 1, :] == here
                nm = jnp.where(hit, 1.0, nm)
                gt = jnp.where(hit, gts[k : k + 1, :], gt)
            m_buf[j * 16 : (j + 1) * 16, :] = nm
            gates[j * 16 : (j + 1) * 16, :] = gt
        bef = dot(m_buf[...].astype(BF), earlier())
        slots[...] = jnp.where(m_buf[...] > 0, bef, 99.0)

        def one(j, carry):
            base = pl.multiple_of(j * 16, 16)
            sl = slots[pl.ds(base, 16), :]
            gt = gates[pl.ds(base, 16), :]
            for s in range(CAP):
                w_buf[j, s * 16 : (s + 1) * 16, :] = jnp.where(sl == float(s), gt, 0.0).astype(BF)
            return carry

        lax.fori_loop(0, 16, one, 0)

    def block(u, zb):
        for i in range(2):
            j = 2 * zb + i
            got = dot(w_buf[j], x_buf[u, j])
            for s in range(CAP):
                f_buf[u % 4, pl.ds(s * 16 + j, 16, stride=CAP * 16), :] = got[s * 16 : (s + 1) * 16, :]

    def place(u, xs, cs):
        cols = pl.ds(pl.multiple_of(cs * 1024 + u * UW, UW), UW)
        return r_buf.at[:, pl.ds(pl.multiple_of(xs * 16, 16), 16), cols]

    out_cp = []

    def rows(u, a):
        dx, dc = REL[a]
        xd, cd = lax.rem(x + dx, NX), lax.rem(c + dc, 2)
        base = pl.multiple_of((xd * 2 + cd) * (ROWS * 16), 32)
        o_buf[u, a] = f_buf[u % 4, pl.ds(base, ROWS * 16), :].astype(BF).reshape(ROWS, 16, UW)
        if a < 7:
            cp = send(o_buf.at[u, a], place(u, x, c), x_s, x_r.at[u], at(dx=dx, dc=dc))
        else:
            cp = pltpu.make_async_copy(o_buf.at[u, a], place(u, x, c), loc.at[15 + u])
            out_cp.append(cp)
        cp.start()

    def across():
        bulk(g2_buf, 6, h_r)
        bulk(mb2, 6, h2_r)
        mb2[pl.ds(2 * x, 2)] = mb[pl.ds(2 * z, 2)]
        here = x * 32 + iota((32, TOK), 0)
        for j in range(8):
            ids = mb2[j, 0:TOP, :].astype(F32).astype(jnp.int32)
            gts = mb2[j, TOP:, :].astype(F32)
            nm = jnp.zeros((32, TOK), F32)
            gt = jnp.zeros((32, TOK), F32)
            for k in range(TOP):
                hit = ids[k : k + 1, :] == here
                nm = jnp.where(hit, 1.0, nm)
                gt = jnp.where(hit, gts[k : k + 1, :], gt)
            m_buf[j * 32 : (j + 1) * 32, :] = nm
            gates[j * 32 : (j + 1) * 32, :] = gt
        bef = dot(m_buf[...].astype(BF), earlier())
        slots[...] = jnp.where(m_buf[...] > 0, bef, 99.0)
        for j in range(8):
            sl = slots[j * 32 : (j + 1) * 32, :]
            gt = gates[j * 32 : (j + 1) * 32, :]
            for s in range(CAP):
                w2_buf[j, s * 32 : (s + 1) * 32, :] = jnp.where(sl == float(s), gt, 0.0).astype(BF)
        for j in range(8):
            got = dot(w2_buf[j], g2_buf[j])
            for s in range(CAP):
                f2_buf[pl.ds(s * 8 + j, 32, stride=CAP * 8), :] = got[s * 32 : (s + 1) * 32, :]
        o2_buf[...] = f2_buf[...].astype(BF).reshape(16, ROWS * 8, UW)
        h_in[pl.ds(2 * z + c, 1)] = o2_buf[pl.ds(2 * z + c, 1)]
        to, fr = iota((128, 128), 0), iota((128, 128), 1)
        q = lax.rem(to, 64)
        want = (lax.rem(q, 16) // 2) * 16 + (to // 64) * 8 + (q // 16) * 2 + lax.rem(q, 2)
        turn[...] = (fr == want).astype(BF)

    h3_cp = []

    def across_send(n):
        for _ in range(n):
            i = len(h3_cp)
            if i == len(zc):
                return
            dz, dc = ACROSS[i]
            to = 2 * lax.rem(z + dz, NZ) + lax.rem(c + dc, 2)
            cp = send(o2_buf.at[to], h_in.at[2 * z + c], h3_s, h3_r, at(dz=dz, dc=dc))
            cp.start()
            h3_cp.append(cp)

    def across_done():
        bulk(h_in, 15, h3_r)
        for t in range(CAP):
            tile = pl.ds(t * 16, 16)
            both = [
                jnp.concatenate([h_in[2 * k + h, tile, :] for k in range(NZ)], axis=0) for h in range(2)
            ]
            got = dot(turn[...], jnp.concatenate(both, axis=1)).astype(BF)
            for h in range(2):
                col = h * 1024 + RING * UW
                r_buf[2 * t : 2 * t + 2, :, col : col + UW] = got[:, h * UW : (h + 1) * UW].reshape(2, 64, UW)

    def work(u, h):
        if h == 0:
            block(u, z)
        for d in range(2):
            if 0 < h <= HOPS[u % 2][d]:
                block(u, came(d, h))
        if h == 4:
            for a in range(8):
                rows(u, a)
            if u == 1:
                across()

    late = [steps[0]]
    for n, (u, h) in enumerate(steps[1:]):
        hop(u, h)
        late.append((u, h))
        across_send(SPREAD.get((u, h), 0))
        if n == 2:
            for cp in li_cp:
                cp.start()
            tables()
        if n >= 2:
            for q in late:
                work(*q)
            late = []

    own_li.wait()
    bulk(lib, 7, li_r)
    eye = (iota((TOK, TOK), 0) == iota((TOK, TOK), 1)).astype(BF)
    for g in range(8):
        lit[:, g * TOK : (g + 1) * TOK] = dot(lib[g], eye, ((0,), (0,))).astype(BF)

    load_e.wait()
    for u in ORDER:
        if u == RING:
            across_done()
        else:
            taken(o_buf.at[u, pl.ds(0, 7)], x_r.at[u])
            out_cp[u].wait()
        for h in range(2):
            cols = pl.ds(h * 1024 + u * UW, UW)
            cp = pltpu.make_async_copy(r_buf.at[:, :, cols], grows.at[:, :, cols], loc.at[0])
            cp.start()

        def score(r, carry, u=u):
            tot = jnp.zeros((64, 128), F32)
            for h in range(2):
                col = h * 1024 + u * UW
                a = r_buf[r, :, col : col + 128].astype(F32)
                b = e_buf[r, :, col : col + 128].astype(F32)
                tot = tot + a * b
            acc[r] = tot if u == 0 else acc[r] + tot
            return carry

        lax.fori_loop(0, ROWS, score, 0)

    total = jnp.zeros((64, 128), F32)
    for r in range(ROWS):
        total = jnp.where(iota((64, 128), 1) == r, jnp.sum(acc[r], axis=1, keepdims=True), total)
    s_out[...] = total

    def sc(i):
        to = lax.rem(idx + i, 64)
        return send(s_out.at[pl.ds(to, 1)], t_in.at[pl.ds(idx, 1)], sc_s, sc_r, (y, to))

    def sc_start(i, carry):
        sc(i).start()
        return carry

    for i in range(1, 64):
        sc_start(i, 0)
    t_in[pl.ds(idx, 1)] = s_out[pl.ds(idx, 1)]
    taken(x_buf.at[:, 0], xch_s)
    taken(x_buf.at[pl.ds(0, RING), pl.ds(0, 14)], ring_s)
    taken(o_buf.at[pl.ds(0, RING), pl.ds(0, 7)], x_s)
    bulk(mb, 15, meta_s)
    bulk(lib, 7, li_s)
    bulk(g2_buf, 6, h_s)
    bulk(mb2, 6, h2_s)
    bulk(h_in, 15, h3_s)
    bulk(mb3, 7, h4_s)
    bulk(mb3, 7, h4_r)
    taken(count, sc_r)

    back = t_in[...]
    scaled = []
    for l in range(2):
        sl = own_slot[l * 64 : (l + 1) * 64, :]
        v = jnp.zeros((64, TOK), F32)
        for s in range(CAP):
            v = jnp.where(sl == float(s), back[:, l * CAP + s : l * CAP + s + 1], v)
        scaled.append(v)
    scaled = jnp.concatenate(scaled, axis=0)
    total = jnp.sum(scaled, axis=0, keepdims=True)
    for k in range(TOP):
        mine = jnp.sum(jnp.where(ids_own[k : k + 1, :] == expert, scaled, 0.0), axis=0, keepdims=True)
        few[k : k + 1, :] = mine - gates_own[k : k + 1, :] * total

    for dy, dc in yc:
        send(few, fews.at[2 * y + c], gl_s, gl_r, at(dy=dy, dc=dc)).start()
    fews[pl.ds(2 * y + c, 1)] = few[...].reshape(1, TOP, TOK)

    def spread(ids, vals):
        got = jnp.zeros((EXP, TOK), F32)
        for k in range(TOP):
            got = jnp.where(ids[k : k + 1, :] == lane_row, vals[k : k + 1, :], got)
        return got.astype(BF)

    glt[...] = spread(ids_own[...], few[...])
    load_rw.wait()
    gin[...] = dot(glt[...], rw[...], ((0,), (1,))).astype(BF)
    pltpu.make_async_copy(gin, gin_out, loc.at[1]).start()
    bulk(fews, 7, gl_r)
    for j in range(8):
        glb[:, j * TOK : (j + 1) * TOK] = spread(mb3[j, 0:TOP, :].astype(F32).astype(jnp.int32), fews[j])
    part[...] = dot(lit[...], glb[...], ((1,), (1,))).astype(BF)

    chip = x * NZ + z
    seat = x * 4 + z // 2
    owner = lax.rem(z, 2) == 0

    def seat_at(q):
        return (y, (q // 4) * 16 + lax.rem(q, 4) * 4 + c)

    def rs_start(i, carry):
        q = lax.rem(seat + i, 16)
        send(
            part.at[pl.ds(pl.multiple_of(q * 16, 16), 16)], rb.at[chip], rs_s, rs_r, seat_at(q)
        ).start()
        return carry

    def a1_start(i, carry):
        q = lax.rem(chip + i, 32)
        send(fin, ag.at[seat], a1_s, a1_r, (y, q * 2 + c)).start()
        return carry

    for i in range(1, 16):
        rs_start(i, 0)

    @pl.when(owner)
    def _():
        rb[pl.ds(chip, 1)] = part[pl.ds(pl.multiple_of(seat * 16, 16), 16), :].reshape(1, 16, EXP)
        taken(count, sc_s)
        bulk(fews, 7, gl_s)
        bulk(rb, 31, rs_r)
        fin[...] = jnp.sum(rb[...].astype(F32), axis=0).astype(BF)
        for i in range(1, 32):
            a1_start(i, 0)
        ag[pl.ds(seat, 1)] = fin[...].reshape(1, 16, EXP)
        bulk(rb, 15, rs_s)
        bulk(ag, 15, a1_r)

    @pl.when(jnp.logical_not(owner))
    def _():
        rs_start(0, 0)
        taken(count, sc_s)
        bulk(fews, 7, gl_s)
        bulk(rb, 16, rs_s)
        bulk(ag, 16, a1_r)

    half[...] = ag[...].reshape(256, EXP)

    for i in range(1, NY):
        cp = send(half, agb.at[2 * y + c], a2_s, a2_r.at[i], at(dy=i))
        cp.start()

    def swap_part(g, src):
        send(src, agb.at[g], a3_s, a3_r, at(dc=1)).start()

    swap_part(2 * y + c, half)
    agb[pl.ds(2 * y + c, 1)] = half[...].reshape(1, 256, EXP)

    @pl.when(owner)
    def _():
        bulk(rb, 31, a1_s)

    taken(r_buf, loc.at[0])
    taken(gin, loc.at[1])
    for i in range(1, NY):
        ys = lax.rem(y + NY - i, NY)
        send(half, agb.at[2 * ys + c], a2_s, a2_r.at[i], at(dy=i)).wait_recv()
        swap_part(2 * ys + c, agb.at[2 * ys + c])
    bulk(agb, NY, a3_r)
    store = pltpu.make_async_copy(agb, agb_out, loc.at[0])
    store.start()
    bulk(agb, NY - 1, a2_s)
    bulk(agb, NY, a3_s)
    store.wait()


def writer(rows_in, gin_in, agb_in, grows, gin_out, grout, rows, gin, parts, wide, loc, sto):
    pieces = [pl.ds(3 * i, 3) for i in range(6)]
    loads = [pltpu.make_async_copy(agb_in, parts, loc.at[6]), pltpu.make_async_copy(gin_in, gin, loc.at[7])]
    loads += [pltpu.make_async_copy(rows_in.at[p], rows.at[p], loc.at[i]) for i, p in enumerate(pieces)]
    for cp in loads:
        cp.start()
    loads[0].wait()
    wide[...] = parts[...].reshape(D, EXP).astype(F32)
    pltpu.make_async_copy(wide, grout, sto.at[0]).start()
    loads[1].wait()
    pltpu.make_async_copy(gin, gin_out, sto.at[1]).start()
    for i, p in enumerate(pieces):
        loads[2 + i].wait()
        pltpu.make_async_copy(rows.at[p], grows.at[p], sto.at[2]).start()
    pltpu.make_async_copy(wide, grout, sto.at[0]).wait()
    pltpu.make_async_copy(gin, gin_out, sto.at[1]).wait()
    pltpu.make_async_copy(rows, grows, sto.at[2]).wait()


def body(grad_out, layer_input, router_weight, gate_probs, expert_ids, expert_out):
    eo = expert_out[0].transpose(0, 2, 1, 3).reshape(ROWS, 64, D)
    vm, sem = pltpu.VMEM, pltpu.SemaphoreType.DMA
    hbm = pl.BlockSpec(memory_space=pltpu.HBM)
    results = pl.pallas_call(
        kernel,
        out_shape=(
            jax.ShapeDtypeStruct((ROWS, 64, D), BF),
            jax.ShapeDtypeStruct((TOK, D), BF),
            jax.ShapeDtypeStruct((8, 256, EXP), BF),
        ),
        in_specs=[hbm] * 6,
        out_specs=(hbm, hbm, hbm),
        scratch_shapes=[
            vm((UNITS, 16, TOK, UW), BF),
            vm((4, 8 * ROWS * 16, UW), F32),
            vm((UNITS, 8, ROWS, 16, UW), BF),
            vm((16, CAP * 16, TOK), BF),
            vm((ROWS, 64, D), BF),
            vm((TOK, D), BF),
            vm((8, 256, EXP), BF),
            vm((ROWS, 64, D), BF),
            vm((D, EXP), BF),
            vm((TOP, TOK), jnp.int32),
            vm((TOP, TOK), F32),
            vm((2 * TOP, TOK), BF),
            vm((16, 2 * TOP, TOK), BF),
            vm((256, TOK), F32),
            vm((256, TOK), F32),
            vm((256, TOK), F32),
            vm((8, 2 * TOP, TOK), BF),
            vm((8, TOK, UW), BF),
            vm((8, CAP * 32, TOK), BF),
            vm((16 * ROWS * 8, UW), F32),
            vm((16, ROWS * 8, UW), BF),
            vm((16, ROWS * 8, UW), BF),
            vm((128, 128), BF),
            vm((8, 2 * TOP, TOK), BF),
            vm((TOP, TOK), F32),
            vm((8, TOP, TOK), F32),
            vm((EXP, TOK), F32),
            vm((EXP, TOK), F32),
            vm((ROWS, 64, 128), F32),
            vm((64, 128), F32),
            vm((64, 128), F32),
            vm((63, 1, 128), F32),
            vm((8, TOK, WID), BF),
            vm((WID, 8 * TOK), BF),
            vm((EXP, TOK), BF),
            vm((EXP, 8 * TOK), BF),
            vm((WID, EXP), BF),
            vm((32, 16, EXP), BF),
            vm((16, EXP), BF),
            vm((16, 16, EXP), BF),
            vm((256, EXP), BF),
            sem((22,)),
            sem, sem((UNITS,)),
            sem, sem((RING + 1, 2, 4)),
            sem, sem,
            sem, sem,
            sem, sem((RING,)),
            sem, sem, sem, sem, sem, sem, sem, sem,
            sem, sem,
            sem, sem,
            sem, sem,
            sem, sem,
            sem, sem((NY,)),
            sem, sem,
        ],
        compiler_params=pltpu.CompilerParams(
            collective_id=0, has_side_effects=True, vmem_limit_bytes=57 * 2**20
        ),
    )(grad_out, layer_input, router_weight, expert_ids.T, gate_probs.T, eo)
    grows, gin, grout = pl.pallas_call(
        writer,
        out_shape=(
            jax.ShapeDtypeStruct((ROWS, 64, D), BF),
            jax.ShapeDtypeStruct((TOK, D), BF),
            jax.ShapeDtypeStruct((D, EXP), F32),
        ),
        in_specs=[hbm] * 3,
        out_specs=(hbm, hbm, hbm),
        scratch_shapes=[
            vm((ROWS, 64, D), BF), vm((TOK, D), BF), vm((8, 256, EXP), BF), vm((D, EXP), F32),
            sem((8,)), sem((3,)),
        ],
        compiler_params=pltpu.CompilerParams(vmem_limit_bytes=57 * 2**20),
    )(*results)
    grows = grows.reshape(2, CAP, 64, D).transpose(0, 2, 1, 3)
    return grows[None], gin, grout


def solution(mesh):
    return jax.shard_map(
        body,
        mesh=mesh,
        in_specs=(
            P(("dp", "expert"), None),
            P(("dp", "expert"), None),
            P(),
            P(("dp", "expert"), None),
            P(("dp", "expert"), None),
            P("dp", "expert", None, None, None),
        ),
        out_specs=(P("dp", "expert", None, None, None), P(("dp", "expert"), None), P()),
        check_vma=False,
    )
```
